256 devices in a mesh: dp: 8 (over x, core), proto: 32 (over z, y).
Axes of the slice: x: 4, y: 4, z: 8, core: 2. Of those that a mesh axis runs over, the one named last changes fastest.
Arguments:
- student_feats: bfloat16 [5120, 256], P(('dp', 'proto')), may hold values from -20 to 20
- teacher_feats: bfloat16 [1024, 256], P(('dp', 'proto')), may hold values from -20 to 20
- prototypes: bfloat16 [256, 65536], P(None, 'proto'), may hold values from -80 to 80
- teacher_prototypes: bfloat16 [256, 65536], P(None, 'proto'), may hold values from -80 to 80
- crop_image: int32 [5120], P('dp'), may hold values from 0 to 511, as said below
- pairing: int32 [5120, 2], P('dp'), may hold values 0 or 1
Outputs:
- student_grad: float32 [5120, 256], P(('dp', 'proto'))
- prototype_grad: float32 [256, 65536], P('dp', 'proto')
The draws below stay inside these ranges and needn't reach their ends.
Inputs may be any that keep to these rules, and one draw needn't show every extreme that they name: `crop_image`: rows j * 64 * 10 to (j + 1) * 64 * 10 - 1 name only images j * 64 to (j + 1) * 64 - 1, each of them exactly 10 times.
All inputs are finite; a program needn't handle non-finite values. No bound on the sum of `pairing` on one device may be relied on, other than what follows from the above.
Results may differ from the reference program's by a relative error of at most 0.012.
The reference program's roundings to bfloat16 on the way (of `student_unit`, `prototype_unit` and `score_grad`) count: a program that leaves them out, or rounds other values in their place, can miss the bound.
Values may be sent and summed in bfloat16 or wider, within the bound.
A program may use at most 64 MiB of HBM per device.

```python
import jax
import jax.numpy as jnp
from jax import lax

BOTTLENECK = 256
PROTO_DEV = 2048
IMG_DEV = 64
GLOBAL = 2
ITERS = 3
VIEWS = 10
IMAGES = 512
STUDENTS = 5120
TEACHERS = 1024
PROTOS = 65536
N_PROTO = 32


def cluster_total():
    return max(IMAGES // 2, 1)


def cluster_centers(key):
    normal_draw = jax.random.normal(jax.random.fold_in(key, 11), (cluster_total(), BOTTLENECK), jnp.float32)
    return jnp.clip(normal_draw, -4.0, 4.0)


def image_clusters(key):
    return jax.random.randint(jax.random.fold_in(key, 13), (IMAGES,), 0, cluster_total()).astype(jnp.int32)


def column_clusters():
    return (jnp.arange(PROTOS, dtype=jnp.int32) * cluster_total() // PROTOS).astype(jnp.int32)


def crop_images(key):
    folded = jax.random.fold_in(key, 17)
    blocks = IMAGES // IMG_DEV
    block_keys = jax.random.split(folded, blocks)

    def shuffled(block_key):
        return jax.random.permutation(block_key, IMG_DEV * VIEWS)
    orders = jax.vmap(shuffled)(block_keys).astype(jnp.int32)
    starting = jnp.arange(blocks, dtype=jnp.int32)[:, None] * IMG_DEV
    return (orders // VIEWS + starting).reshape(-1).astype(jnp.int32)


def log_scales(key, amount, lowest, highest):
    return jnp.exp(jax.random.uniform(key, (amount,), jnp.float32, jnp.log(lowest), jnp.log(highest)))


def draw_crop_image(key, part):
    images = crop_images(key)
    return images


def draw_prototypes(key, part):
    middle = cluster_centers(key)
    key = jax.random.fold_in(key, 21)
    noise_key, scale_key = jax.random.split(key)
    extent = (BOTTLENECK, PROTOS)
    jitter = 0.5 * jnp.clip(jax.random.normal(noise_key, extent, jnp.float32), -4.0, 4.0)
    scales = log_scales(scale_key, PROTOS, 1.0, 10.0)
    picked = jnp.take(middle, column_clusters(), axis=0).T
    return ((picked + jitter) * scales[None, :]).astype(jnp.bfloat16)


def draw_teacher_prototypes(key, part):
    middle = cluster_centers(key)
    key = jax.random.fold_in(key, 23)
    noise_key, scale_key = jax.random.split(key)
    extent = (BOTTLENECK, PROTOS)
    jitter = 0.5 * jnp.clip(jax.random.normal(noise_key, extent, jnp.float32), -4.0, 4.0)
    scales = log_scales(scale_key, PROTOS, 1.0, 10.0)
    picked = jnp.take(middle, column_clusters(), axis=0).T
    return ((picked + jitter) * scales[None, :]).astype(jnp.bfloat16)


def draw_teacher_feats(key, part):
    middle = cluster_centers(key)
    owners = image_clusters(key)
    key = jax.random.fold_in(key, 31)
    noise_key, scale_key = jax.random.split(key)
    extent = (TEACHERS, BOTTLENECK)
    jitter = 0.5 * jnp.clip(jax.random.normal(noise_key, extent, jnp.float32), -4.0, 4.0)
    scales = log_scales(scale_key, TEACHERS, 0.5, 2.0)
    row_owner = jnp.repeat(owners, GLOBAL).astype(jnp.int32)
    centered = jnp.take(middle, row_owner, axis=0)
    return ((centered + jitter) * scales[:, None]).astype(jnp.bfloat16)


def draw_student_feats(key, part):
    middle = cluster_centers(key)
    owners = image_clusters(key)
    images = crop_images(key)
    key = jax.random.fold_in(key, 37)
    noise_key, scale_key = jax.random.split(key)
    extent = (STUDENTS, BOTTLENECK)
    jitter = 0.5 * jnp.clip(jax.random.normal(noise_key, extent, jnp.float32), -4.0, 4.0)
    scales = log_scales(scale_key, STUDENTS, 0.5, 2.0)
    row_owner = jnp.take(owners, images, axis=0).astype(jnp.int32)
    centered = jnp.take(middle, row_owner, axis=0)
    return ((centered + jitter) * scales[:, None]).astype(jnp.bfloat16)


def touch_ends(drawn, key, least, largest):
    longest = drawn.shape.index(max(drawn.shape))
    spots = []
    for shift in (0, 1):
        where = [jax.random.randint(jax.random.fold_in(key, axis), (), 0, length) for axis, length in enumerate(drawn.shape)]
        where[longest] = (where[longest] + shift) % drawn.shape[longest]
        spots.append(tuple(where))
    return drawn.at[spots[0]].set(least).at[spots[1]].set(largest)


def setup_inputs(seed: int = 0) -> dict:
    keys = jax.random.split(jax.random.key(seed), 7)
    return {
        "student_feats": draw_student_feats(jax.random.fold_in(keys[6], 71), 0),
        "teacher_feats": draw_teacher_feats(jax.random.fold_in(keys[6], 71), 0),
        "prototypes": draw_prototypes(jax.random.fold_in(keys[6], 71), 0),
        "teacher_prototypes": draw_teacher_prototypes(jax.random.fold_in(keys[6], 71), 0),
        "crop_image": draw_crop_image(jax.random.fold_in(keys[6], 71), 0),
        "pairing": touch_ends((jax.random.randint(keys[5], (STUDENTS, GLOBAL), 0, 4) < 3).astype(jnp.int32), jax.random.fold_in(keys[5], 1), 0, 1),
    }


epsilon = 1e-06
teacher_temp = 0.07
student_temp = 0.1
loss_scale = 4096.0

def unit_rows(values):
    widened = values.astype(jnp.float32)
    length = jnp.sqrt(lax.optimization_barrier(jnp.sum(widened * widened, axis=1, keepdims=True)) + epsilon)
    return (length, widened / length)

def unit_columns(values):
    widened = values.astype(jnp.float32)
    length = jnp.sqrt(lax.optimization_barrier(jnp.sum(widened * widened, axis=0, keepdims=True)) + epsilon)
    return (length, widened / length)

def reference(student_feats, teacher_feats, prototypes, teacher_prototypes, crop_image, pairing):
    student_norm, student_dir = unit_rows(student_feats)
    student_unit = student_dir.astype(jnp.bfloat16)
    teacher_unit = unit_rows(teacher_feats)[1].astype(jnp.bfloat16)
    prototype_norm, prototype_dir = unit_columns(prototypes)
    prototype_unit = prototype_dir.astype(jnp.bfloat16)
    teacher_proto_unit = unit_columns(teacher_prototypes)[1].astype(jnp.bfloat16)
    student_blocks = prototype_unit.reshape(BOTTLENECK, N_PROTO, PROTO_DEV).transpose(1, 0, 2)
    teacher_blocks = teacher_proto_unit.reshape(BOTTLENECK, N_PROTO, PROTO_DEV).transpose(1, 0, 2)

    def teacher_exp(proto_block):
        return jnp.exp(jnp.dot(teacher_unit, proto_block, preferred_element_type=jnp.float32) / teacher_temp)
    row_scale = jnp.ones((TEACHERS,), jnp.float32)
    column_scale = jnp.ones((N_PROTO, PROTO_DEV), jnp.float32)
    for iteration in range(ITERS):

        def column_pass(proto_block, rows_now=row_scale):
            weighted = teacher_exp(proto_block)
            scale_cols = 1.0 / lax.optimization_barrier(jnp.sum(weighted * rows_now[:, None], axis=0))
            return (scale_cols, lax.optimization_barrier(jnp.sum(weighted * scale_cols[None, :], axis=1)))
        column_scale, row_parts = lax.map(column_pass, teacher_blocks)
        row_scale = 1.0 / lax.optimization_barrier(jnp.sum(row_parts, axis=0))

    def student_mass(proto_block):
        scores = jnp.dot(student_unit, proto_block, preferred_element_type=jnp.float32) / student_temp
        return lax.optimization_barrier(jnp.sum(jnp.exp(scores), axis=1))
    totals = lax.optimization_barrier(jnp.sum(lax.map(student_mass, student_blocks), axis=0))
    weights = pairing.astype(jnp.float32)
    counts = lax.optimization_barrier(jnp.sum(weights, axis=1))

    def grad_step(running, slices):
        proto_block, teacher_block, scale_cols = slices
        scores = jnp.dot(student_unit, proto_block, preferred_element_type=jnp.float32) / student_temp
        probability = jnp.exp(scores) / totals[:, None]
        assignment = teacher_exp(teacher_block) * scale_cols[None, :] * row_scale[:, None]
        targets = jnp.zeros_like(probability)
        for view_index in range(GLOBAL):
            picked = jnp.take(assignment, (crop_image * GLOBAL + view_index).astype(jnp.int32), axis=0)
            targets = targets + weights[:, view_index:view_index + 1] * picked
        score_grad = (loss_scale / student_temp * (counts[:, None] * probability - targets)).astype(jnp.bfloat16)
        running = running + jnp.dot(score_grad, proto_block.T, preferred_element_type=jnp.float32)
        return (running, jnp.dot(student_unit.T, score_grad, preferred_element_type=jnp.float32))
    unit_grad, proto_parts = lax.scan(grad_step, jnp.zeros((STUDENTS, BOTTLENECK), jnp.float32), (student_blocks, teacher_blocks, column_scale))
    proto_unit_grad = proto_parts.transpose(1, 0, 2).reshape(BOTTLENECK, PROTOS)
    student_grad = (unit_grad - student_dir * lax.optimization_barrier(jnp.sum(student_dir * unit_grad, axis=1, keepdims=True))) / student_norm
    prototype_grad = (proto_unit_grad - prototype_dir * lax.optimization_barrier(jnp.sum(prototype_dir * proto_unit_grad, axis=0, keepdims=True))) / prototype_norm
    return (student_grad, prototype_grad)
```

```python
import jax
import jax.numpy as jnp
from jax import lax
from jax.experimental import pallas as pl
from jax.experimental.pallas import tpu as pltpu
from jax.sharding import PartitionSpec as P

MESH = pl.DeviceIdType.MESH
F32 = jnp.float32
BF16 = jnp.bfloat16

IMG_DEV = 64
EPS = 1e-06
TEACHER_SCALE = 1.0 / 0.07
STUDENT_SCALE = 1.0 / 0.1
GRAD_SCALE = 4096.0 / 0.1

NDP = 8
NPR = 32
K = 256
C = 2048
R = 640
T = 128
OWN = 20
PAD = 48
HPAD = 40
CH = 512

(X_TEACH, X_STUD, X_COL1, X_TGRP, X_ROW1, X_A1, X_TOT, X_ROW2, X_H, X_UT, X_ROW3, X_G, X_PG, X_GALL, X_DOT) = range(15)
N_X = 15


def row_to_columns(row):
    return jnp.transpose(jnp.broadcast_to(row, (128, 128)))


def columns_to_row(part):
    return jnp.sum(jnp.transpose(part), axis=0, keepdims=True)


def lane_tiles(value):
    total = value[:, 0:128]
    for j in range(1, value.shape[1] // 128):
        total = total + value[:, 128 * j : 128 * j + 128]
    return total


def dot(a, b):
    return jnp.dot(a, b, preferred_element_type=F32)


def dot_nt(a, b):
    return lax.dot_general(a, b, (((1,), (1,)), ((), ())), preferred_element_type=F32)


def kernel(
    sf, tf, pr, tp, crop, pair,
    sgrad, pgrad,
    teach, stud, col1, tgrp, row1, a1, tot, row2, hbuf, utbuf, row3, gbuf, pgbuf, gall, dotbuf,
    hsend, utsend, gsend, pgsend,
    pack, x32, xb, xt, wb, tpb, pnorm, expo, expb, probb, selb, scalec, harr, garr, ass, assb, cvec, avec,
    sdir, snorm, ownsel,
    ssem, rsem,
):
    dp = lax.axis_index("dp")
    pi = lax.axis_index("proto")

    def peer(axis, i):
        if axis == "dp":
            return lax.rem(dp + i + 1, NDP), NDP - 1
        zi, yi = i // 4, lax.rem(i, 4)
        dz = 4 + ((zi + 1) // 2) * (1 - 2 * lax.rem(zi, 2))
        dy = 2 + ((yi + 1) // 2) * (1 - 2 * lax.rem(yi, 2))
        z = lax.rem(pi // 4 + dz, 8)
        y = lax.rem(lax.rem(pi, 4) + dy, 4)
        return z * 4 + y, NPR - 1

    def address(axis, p):
        return (p, pi) if axis == "dp" else (dp, p)

    def mine(axis):
        return dp if axis == "dp" else pi

    def count(axis):
        return NDP if axis == "dp" else NPR

    def send(x, axis, dst, src=None):
        me = mine(axis)

        @pl.loop(0, count(axis) - 1)
        def _(i):
            p, _n = peer(axis, i)
            pltpu.make_async_remote_copy(
                src_ref=dst.at[me] if src is None else src.at[p],
                dst_ref=dst.at[me],
                send_sem=ssem.at[x],
                recv_sem=rsem.at[x],
                device_id=address(axis, p),
                device_id_type=MESH,
            ).start()

    def arrived(x, axis, dst):
        blocks = dst.at[pl.ds(0, count(axis) - 1)]
        pltpu.make_async_copy(blocks, blocks, rsem.at[x]).wait()

    def sent(x, axis, dst):
        blocks = dst.at[pl.ds(0, count(axis) - 1)]
        pltpu.make_async_copy(blocks, blocks, ssem.at[x]).wait()

    def group_rows(g):
        return pl.ds(pl.multiple_of(g * T, T), T)

    barrier = pltpu.get_barrier_semaphore()
    for axis in ("proto", "dp"):
        @pl.loop(0, count(axis) - 1)
        def _(i, axis=axis):
            p, _n = peer(axis, i)
            pl.semaphore_signal(barrier, inc=1, device_id=address(axis, p), device_id_type=MESH)

    tw = tf[...].astype(F32)
    tu = tw / jnp.sqrt(jnp.sum(tw * tw, axis=1, keepdims=True) + EPS)
    teach[pi, 0:4, :] = tu[:, 0:128].astype(BF16).astype(F32)
    teach[pi, 4:8, :] = tu[:, 128:256].astype(BF16).astype(F32)
    sw = sf[...].astype(F32)
    sn = jnp.sqrt(jnp.sum(sw * sw, axis=1, keepdims=True) + EPS)
    sd = sw / sn
    snorm[...] = jnp.broadcast_to(sn, (OWN, 128))
    sdir[...] = sd
    pack[...] = jnp.zeros_like(pack)
    pack[0:OWN, :] = sd[:, 0:128]
    pack[24 : 24 + OWN, :] = sd[:, 128:256]
    stud[pi] = pack[...].astype(BF16)

    @pl.loop(0, C // 256)
    def _(j):
        cols = pl.ds(pl.multiple_of(j * 256, 256), 256)
        v = tp[:, cols].astype(F32)
        inv = 1.0 / jnp.sqrt(jnp.sum(v * v, axis=0, keepdims=True) + EPS)
        tpb[:, cols] = (v * inv).astype(BF16)

    pl.semaphore_wait(barrier, NPR - 1 + NDP - 1)
    send(X_TEACH, "proto", teach)
    send(X_STUD, "proto", stud)

    @pl.loop(0, C // 256)
    def _(j):
        cols = pl.ds(pl.multiple_of(j * 256, 256), 256)
        v = pr[:, cols].astype(F32)
        n = jnp.sqrt(jnp.sum(v * v, axis=0, keepdims=True) + EPS)
        pnorm[:, cols] = n
        wb[:, cols] = (v * (1.0 / n)).astype(BF16)

    lanes = lax.broadcasted_iota(jnp.int32, (128, 128), 1).astype(F32)
    base = (dp * IMG_DEV).astype(F32)
    for i in range(R // 128):
        image = row_to_columns(crop[i : i + 1, :].astype(F32)) - base
        w = pair[128 * i : 128 * i + 128, :].astype(F32)
        sel = jnp.where(lanes == 2.0 * image, w[:, 0:1], 0.0) + jnp.where(lanes == 2.0 * image + 1.0, w[:, 1:2], 0.0)
        selb[128 * i : 128 * i + 128, :] = sel.astype(BF16)
        scalec[128 * i : 128 * i + 128, :] = jnp.broadcast_to(w[:, 0:1] + w[:, 1:2], (128, 128))
    own_rows = lax.broadcasted_iota(jnp.int32, (32, R), 0) + pi * OWN
    ownsel[...] = (lax.broadcasted_iota(jnp.int32, (32, R), 1) == own_rows).astype(F32)

    arrived(X_TEACH, "proto", teach)
    for p in range(NPR):
        v = teach[p]
        x32[4 * p : 4 * p + 4, 0:128] = v[0:4]
        x32[4 * p : 4 * p + 4, 128:256] = v[4:8]
    tgrp[dp] = x32[0:T, :].astype(BF16)

    def assign(g):
        rows = tgrp[g]
        for j in range(C // CH):
            e = jnp.exp(dot(rows, tpb[:, CH * j : CH * j + CH]) * TEACHER_SCALE)
            ass[group_rows(g), CH * j : CH * j + CH] = e
            assb[group_rows(g), CH * j : CH * j + CH] = e.astype(BF16)

    assign(dp)

    def column_part(g, acc, arow):
        if arow is not None:
            wide = row_to_columns(arow)
        for i in range(T // 8):
            e = ass[pl.ds(pl.multiple_of(g * T + 8 * i, 8), 8), :]
            if arow is not None:
                e = e * jnp.concatenate([wide[8 * i : 8 * i + 8]] * (C // 128), axis=1)
            acc = acc + e
        return acc

    def row_part(g):
        cb = jnp.broadcast_to(cvec[...], (8, C))
        parts = []
        for i in range(T // 8):
            parts.append(lane_tiles(ass[pl.ds(pl.multiple_of(g * T + 8 * i, 8), 8), :] * cb))
        return columns_to_row(jnp.concatenate(parts, axis=0))

    col1[dp] = jnp.sum(column_part(dp, jnp.zeros((8, C), F32), None), axis=0, keepdims=True)
    send(X_COL1, "dp", col1)
    send(X_TGRP, "dp", tgrp)

    arrived(X_COL1, "dp", col1)
    cvec[...] = 1.0 / jnp.sum(col1[...], axis=0)
    row1[pi] = row_part(dp)
    send(X_ROW1, "proto", row1)

    arrived(X_STUD, "proto", stud)
    for p in range(NPR):
        v = stud[p].astype(F32)
        x32[OWN * p : OWN * p + OWN, 0:128] = v[0:OWN]
        x32[OWN * p : OWN * p + OWN, 128:256] = v[24 : 24 + OWN]
    xb[...] = x32[...].astype(BF16)
    for i in range(R // 128):
        xt[:, 128 * i : 128 * i + 128] = jnp.transpose(x32[128 * i : 128 * i + 128, :]).astype(BF16)

    @pl.loop(0, R // 128)
    def _(i):
        rows = pl.ds(pl.multiple_of(i * 128, 128), 128)
        part = jnp.zeros((128, 128), F32)
        for j in range(C // CH):
            e = jnp.exp(dot(xb[rows, :], wb[:, CH * j : CH * j + CH]) * STUDENT_SCALE)
            expo[rows, CH * j : CH * j + CH] = e
            expb[rows, CH * j : CH * j + CH] = e.astype(BF16)
            part = part + lane_tiles(e)
        tot[pi, pl.ds(i, 1), :] = columns_to_row(part)

    tot[pi, 5:8, :] = jnp.ones((3, 128), F32)

    arrived(X_ROW1, "proto", row1)
    a1[dp] = 1.0 / jnp.sum(row1[...], axis=0)
    send(X_A1, "dp", a1)
    send(X_TOT, "proto", tot)

    arrived(X_TGRP, "dp", tgrp)

    @pl.loop(1, NDP)
    def _(i):
        assign(lax.rem(dp + i, NDP))

    arrived(X_A1, "dp", a1)
    for g in range(NDP):
        avec[g : g + 1, :] = a1[g]

    def columns():
        acc = lax.fori_loop(
            0, NDP, lambda g, acc: column_part(g, acc, avec[pl.ds(g, 1), :]), jnp.zeros((8, C), F32)
        )
        cvec[...] = 1.0 / jnp.sum(acc, axis=0, keepdims=True)

    def rows_into(buf):
        @pl.loop(0, NDP)
        def _(g):
            buf[pi, pl.ds(g, 1), :] = row_part(g)

    columns()
    rows_into(row2)
    send(X_ROW2, "proto", row2)

    @pl.loop(0, R // 128)
    def _(i):
        rows = pl.ds(pl.multiple_of(i * 128, 128), 128)
        harr[rows, :] = dot_nt(expb[rows, :], wb[...])

    for p in range(NPR):
        hsend[p, 0:OWN, :] = harr[OWN * p : OWN * p + OWN, 0:128]
        hsend[p, OWN:HPAD, :] = harr[OWN * p : OWN * p + OWN, 128:256]
    send(X_H, "proto", hbuf, hsend)
    hbuf[pi] = hsend[pi]

    ut = dot(xt[...], selb[...])
    for g in range(NDP):
        utsend[g] = ut[32 * g : 32 * g + 32, :]
    send(X_UT, "dp", utbuf, utsend)
    utbuf[dp] = utsend[dp]

    arrived(X_TOT, "proto", tot)
    inv_tot = 1.0 / jnp.sum(tot[...], axis=0)
    for i in range(R // 128):
        rows = slice(128 * i, 128 * i + 128)
        scalec[rows, :] = scalec[rows, :] * row_to_columns(inv_tot[i : i + 1, :])

    @pl.loop(0, R // 16)
    def _(i):
        rows = pl.ds(pl.multiple_of(i * 16, 16), 16)
        s = scalec[rows, :]
        probb[rows, :] = (expo[rows, :] * jnp.concatenate([s] * (C // 128), axis=1)).astype(BF16)

    for j in range(C // CH):
        cols = slice(CH * j, CH * j + CH)
        pg = dot(xt[...], probb[:, cols])
        direction = pr[:, cols].astype(F32) / pnorm[:, cols]
        pg = (pg - direction * jnp.sum(direction * pg, axis=0, keepdims=True)).astype(BF16)
        for g in range(NDP):
            pgsend[g, :, cols] = pg[32 * g : 32 * g + 32, :]
    send(X_PG, "dp", pgbuf, pgsend)
    pgbuf[dp] = pgsend[dp]

    arrived(X_ROW2, "proto", row2)
    avec[...] = 1.0 / jnp.sum(row2[...], axis=0)
    columns()
    rows_into(row3)
    send(X_ROW3, "proto", row3)

    cb = jnp.broadcast_to(cvec[...], (16, C))
    for i in range(T // 16):
        rows = pl.ds(pl.multiple_of(dp * T + 16 * i, 16), 16)
        probb[16 * i : 16 * i + 16, :] = (ass[rows, :] * cb).astype(BF16)
    garr[...] = dot_nt(probb[0:T, :], wb[...])
    for p in range(16):
        gsend[p] = garr[8 * p : 8 * p + 8, 0:128]
        gsend[p + 16] = garr[8 * p : 8 * p + 8, 128:256]
    send(X_G, "proto", gbuf, gsend)
    gbuf[pi] = gsend[pi]

    arrived(X_H, "proto", hbuf)
    hsum = jnp.sum(hbuf[...], axis=0)
    own_scale = jnp.dot(ownsel[...], scalec[...], precision=lax.Precision.HIGHEST, preferred_element_type=F32)[0:OWN, 0:1]
    own_pick = dot(ownsel[...].astype(BF16), selb[...])[0:OWN, :]

    arrived(X_G, "proto", gbuf)
    gall[pi] = jnp.sum(gbuf[...], axis=0)
    send(X_GALL, "proto", gall)

    arrived(X_ROW3, "proto", row3)
    avec[...] = 1.0 / jnp.sum(row3[...], axis=0)
    arrived(X_UT, "dp", utbuf)
    lhs = jnp.concatenate([utbuf[g] * avec[g : g + 1, :] for g in range(NDP)], axis=1)
    high = lhs.astype(BF16)
    lhs = jnp.concatenate([high, (lhs - high.astype(F32)).astype(BF16)], axis=0)
    arrived(X_PG, "dp", pgbuf)
    own32 = pl.ds(pl.multiple_of(dp * 32, 32), 32)
    for j in range(C // CH):
        cols = slice(CH * j, CH * j + CH)
        both = dot(lhs, assb[:, cols])
        target = (both[0:32] + both[32:64]) * cvec[:, cols]
        own = GRAD_SCALE * (jnp.sum(pgbuf[:, :, cols].astype(F32), axis=0) - target)
        own_dir = pr[own32, cols].astype(F32) / pnorm[:, cols]
        pgrad[:, cols] = own
        dotbuf[dp, :, cols] = jnp.sum(own * own_dir, axis=0, keepdims=True)
    send(X_DOT, "dp", dotbuf)

    arrived(X_GALL, "proto", gall)
    gfull = jnp.concatenate([gall[0:16].reshape(T, 128), gall[16:32].reshape(T, 128)], axis=1)
    picked = jnp.dot(
        own_pick * avec[pl.ds(dp, 1), :], gfull, precision=lax.Precision.HIGHEST, preferred_element_type=F32
    )
    h = jnp.concatenate([hsum[0:OWN], hsum[OWN:HPAD]], axis=1)
    unit_grad = GRAD_SCALE * (own_scale * h - picked)
    sd = sdir[...]
    sgrad[...] = (unit_grad - sd * jnp.sum(sd * unit_grad, axis=1, keepdims=True)) / snorm[:, 0:1]

    arrived(X_DOT, "dp", dotbuf)
    column_dot = jnp.sum(dotbuf[...], axis=0)
    for j in range(C // CH):
        cols = slice(CH * j, CH * j + CH)
        n = pnorm[:, cols]
        own_dir = pr[own32, cols].astype(F32) / n
        pgrad[:, cols] = (pgrad[:, cols] - own_dir * column_dot[:, cols]) / n

    for x, axis, buf in (
        (X_TEACH, "proto", teach), (X_STUD, "proto", stud), (X_COL1, "dp", col1), (X_TGRP, "dp", tgrp),
        (X_ROW1, "proto", row1), (X_A1, "dp", a1), (X_TOT, "proto", tot), (X_ROW2, "proto", row2),
        (X_H, "proto", hbuf), (X_UT, "dp", utbuf), (X_ROW3, "proto", row3), (X_G, "proto", gbuf),
        (X_PG, "dp", pgbuf), (X_GALL, "proto", gall), (X_DOT, "dp", dotbuf),
    ):
        sent(x, axis, buf)


def per_device(student_feats, teacher_feats, prototypes, teacher_prototypes, crop_image, pairing):
    vmem = pl.BlockSpec(memory_space=pltpu.VMEM)
    return pl.pallas_call(
        kernel,
        out_shape=(jax.ShapeDtypeStruct((OWN, K), F32), jax.ShapeDtypeStruct((K // NDP, C), F32)),
        in_specs=[vmem] * 6,
        out_specs=(vmem, vmem),
        scratch_shapes=[
            pltpu.VMEM((NPR, 8, 128), F32),
            pltpu.VMEM((NPR, PAD, 128), BF16),
            pltpu.VMEM((NDP, 1, C), F32),
            pltpu.VMEM((NDP, T, K), BF16),
            pltpu.VMEM((NPR, 1, 128), F32),
            pltpu.VMEM((NDP, 1, 128), F32),
            pltpu.VMEM((NPR, 8, 128), F32),
            pltpu.VMEM((NPR, 8, 128), F32),
            pltpu.VMEM((NPR, HPAD, 128), F32),
            pltpu.VMEM((NDP, 32, 128), F32),
            pltpu.VMEM((NPR, 8, 128), F32),
            pltpu.VMEM((NPR, 8, 128), F32),
            pltpu.VMEM((NDP, 32, C), BF16),
            pltpu.VMEM((NPR, 8, 128), F32),
            pltpu.VMEM((NDP, 1, C), F32),
            pltpu.VMEM((NPR, HPAD, 128), F32),
            pltpu.VMEM((NDP, 32, 128), F32),
            pltpu.VMEM((NPR, 8, 128), F32),
            pltpu.VMEM((NDP, 32, C), BF16),
            pltpu.VMEM((PAD, 128), F32),
            pltpu.VMEM((R, K), F32),
            pltpu.VMEM((R, K), BF16),
            pltpu.VMEM((K, R), BF16),
            pltpu.VMEM((K, C), BF16),
            pltpu.VMEM((K, C), BF16),
            pltpu.VMEM((1, C), F32),
            pltpu.VMEM((R, C), F32),
            pltpu.VMEM((R, C), BF16),
            pltpu.VMEM((R, C), BF16),
            pltpu.VMEM((R, 128), BF16),
            pltpu.VMEM((R, 128), F32),
            pltpu.VMEM((R, K), F32),
            pltpu.VMEM((T, K), F32),
            pltpu.VMEM((NDP * T, C), F32),
            pltpu.VMEM((NDP * T, C), BF16),
            pltpu.VMEM((1, C), F32),
            pltpu.VMEM((8, 128), F32),
            pltpu.VMEM((OWN, K), F32),
            pltpu.VMEM((OWN, 128), F32),
            pltpu.VMEM((32, R), F32),
            pltpu.SemaphoreType.DMA((N_X,)),
            pltpu.SemaphoreType.DMA((N_X,)),
        ],
        compiler_params=pltpu.CompilerParams(
            collective_id=0, has_side_effects=True, vmem_limit_bytes=56 * 2**20
        ),
    )(student_feats, teacher_feats, prototypes, teacher_prototypes, crop_image.reshape(R // 128, 128), pairing)


def solution(mesh):
    in_specs = (
        P(("dp", "proto"), None),
        P(("dp", "proto"), None),
        P(None, "proto"),
        P(None, "proto"),
        P("dp"),
        P("dp", None),
    )
    out_specs = (P(("dp", "proto"), None), P("dp", "proto"))
    return jax.shard_map(
        per_device, mesh=mesh, in_specs=in_specs, out_specs=out_specs, check_vma=False
    )
```

```python
import jax
import jax.numpy as jnp
from jax import lax
from jax.experimental import pallas as pl
from jax.experimental.pallas import tpu as pltpu
from jax.sharding import PartitionSpec as P

MESH = pl.DeviceIdType.MESH
F32 = jnp.float32
BF16 = jnp.bfloat16

IMG_DEV = 64
EPS = 1e-06
TEACHER_SCALE = 1.0 / 0.07
STUDENT_SCALE = 1.0 / 0.1
GRAD_SCALE = 4096.0 / 0.1

NDP = 8
NPR = 32
K = 256
C = 2048
R = 640
T = 128
OWN = 20
PAD = 48
HPAD = 40
CH = 512

(
    X_TEACH, X_STUDZ, X_STUDY, X_COL1, X_TGRP, X_ROW1, X_COL2, X_TOT, X_ROW2, X_HY, X_HZ, X_UT, X_ROW3, X_G, X_PG, X_GALL, X_DOT
) = range(17)
N_X = 17
SIZES = {"dp": 8, "proto": 32, "z": 8, "y": 4}


def row_to_columns(row):
    return jnp.transpose(jnp.broadcast_to(row, (128, 128)))


def columns_to_row(part):
    return jnp.sum(jnp.transpose(part), axis=0, keepdims=True)


def lane_tiles(value):
    total = value[:, 0:128]
    for j in range(1, value.shape[1] // 128):
        total = total + value[:, 128 * j : 128 * j + 128]
    return total


def dot(a, b):
    return jnp.dot(a, b, preferred_element_type=F32)


def dot_nt(a, b):
    return lax.dot_general(a, b, (((1,), (1,)), ((), ())), preferred_element_type=F32)


def kernel(
    sfh, tfh, prh, tph, croph, pairh,
    sgrad, pown, pdir, pdot, pnorm,
    teach, stud, col1, tgrp, row1, col2, tot, row2, hybuf, hzbuf, utbuf, row3, gbuf, pgbuf, gall, dotbuf,
    hsend, hzsend, utsend, gsend, pgsend,
    pack, x32, xb, xt, wb, tpb, expo, expb, probb, selb, scalec, harr, garr, ass, assb, cvec, avec,
    sdir, snorm, ownsel, sf, tf, pr, tp, crop, pair,
    ssem, rsem, lsem,
):
    dp = lax.axis_index("dp")
    pi = lax.axis_index("proto")

    pz, py = pi // 4, lax.rem(pi, 4)

    def far_first(i, half):
        return half + ((i + 1) // 2) * (1 - 2 * lax.rem(i, 2))

    def peer(axis, i):
        if axis == "dp":
            return lax.rem(dp + i + 1, NDP)
        if axis == "z":
            return lax.rem(pz + far_first(i, 4), 8)
        if axis == "y":
            return lax.rem(py + far_first(i, 2), 4)
        return lax.rem(pz + far_first(i // 4, 4), 8) * 4 + lax.rem(py + far_first(lax.rem(i, 4), 2), 4)

    def address(axis, p):
        if axis == "dp":
            return (p, pi)
        if axis == "z":
            return (dp, p * 4 + py)
        if axis == "y":
            return (dp, pz * 4 + p)
        return (dp, p)

    def mine(axis):
        return {"dp": dp, "proto": pi, "z": pz, "y": py}[axis]

    def count(axis):
        return SIZES[axis]

    def send(x, axis, dst, src=None):
        me = mine(axis)

        @pl.loop(0, count(axis) - 1)
        def _(i):
            p = peer(axis, i)
            pltpu.make_async_remote_copy(
                src_ref=dst.at[me] if src is None else src.at[p],
                dst_ref=dst.at[me],
                send_sem=ssem.at[x],
                recv_sem=rsem.at[x],
                device_id=address(axis, p),
                device_id_type=MESH,
            ).start()

    def arrived(x, axis, dst):
        blocks = dst.at[pl.ds(0, count(axis) - 1)]
        pltpu.make_async_copy(blocks, blocks, rsem.at[x]).wait()

    def sent(x, axis, dst):
        blocks = dst.at[pl.ds(0, count(axis) - 1)]
        pltpu.make_async_copy(blocks, blocks, ssem.at[x]).wait()

    def group_rows(g):
        return pl.ds(pl.multiple_of(g * T, T), T)

    barrier = pltpu.get_barrier_semaphore()
    for axis in ("proto", "dp"):
        @pl.loop(0, count(axis) - 1)
        def _(i, axis=axis):
            p = peer(axis, i)
            pl.semaphore_signal(barrier, inc=1, device_id=address(axis, p), device_id_type=MESH)

    loads = []
    for k, (src, dst) in enumerate(
        ((tfh, tf), (sfh, sf), (tph, tp), (prh, pr), (croph, crop), (pairh, pair))
    ):
        loads.append(pltpu.make_async_copy(src, dst, lsem.at[k]))
        loads[-1].start()

    loads[0].wait()
    tw = tf[...].astype(F32)
    tu = tw / jnp.sqrt(jnp.sum(tw * tw, axis=1, keepdims=True) + EPS)
    teach[pi, 0:4, :] = tu[:, 0:128].astype(BF16).astype(F32)
    teach[pi, 4:8, :] = tu[:, 128:256].astype(BF16).astype(F32)
    loads[1].wait()
    sw = sf[...].astype(F32)
    sn = jnp.sqrt(jnp.sum(sw * sw, axis=1, keepdims=True) + EPS)
    sd = sw / sn
    snorm[...] = jnp.broadcast_to(sn, (OWN, 128))
    sdir[...] = sd
    pack[...] = jnp.zeros_like(pack)
    pack[0:OWN, :] = sd[:, 0:128]
    pack[24 : 24 + OWN, :] = sd[:, 128:256]
    stud[py, pz] = pack[...].astype(BF16)

    loads[2].wait()

    @pl.loop(0, C // 256)
    def _(j):
        cols = pl.ds(pl.multiple_of(j * 256, 256), 256)
        v = tp[:, cols].astype(F32)
        inv = 1.0 / jnp.sqrt(jnp.sum(v * v, axis=0, keepdims=True) + EPS)
        tpb[:, cols] = (v * inv).astype(BF16)

    pl.semaphore_wait(barrier, NPR - 1 + NDP - 1)
    send(X_TEACH, "proto", teach)
    send(X_STUDZ, "z", stud.at[py])

    loads[3].wait()

    @pl.loop(0, C // 256)
    def _(j):
        cols = pl.ds(pl.multiple_of(j * 256, 256), 256)
        v = pr[:, cols].astype(F32)
        n = jnp.sqrt(jnp.sum(v * v, axis=0, keepdims=True) + EPS)
        pnorm[:, cols] = n
        wb[:, cols] = (v * (1.0 / n)).astype(BF16)

    loads[4].wait()
    loads[5].wait()
    lanes = lax.broadcasted_iota(jnp.int32, (128, 128), 1).astype(F32)
    base = (dp * IMG_DEV).astype(F32)
    for i in range(R // 128):
        image = row_to_columns(crop[i : i + 1, :].astype(F32)) - base
        w0 = row_to_columns(pair[0:1, 128 * i : 128 * i + 128].astype(F32))
        w1 = row_to_columns(pair[1:2, 128 * i : 128 * i + 128].astype(F32))
        sel = jnp.where(lanes == 2.0 * image, w0, 0.0) + jnp.where(lanes == 2.0 * image + 1.0, w1, 0.0)
        selb[128 * i : 128 * i + 128, :] = sel.astype(BF16)
        scalec[128 * i : 128 * i + 128, :] = w0 + w1
    own_rows = lax.broadcasted_iota(jnp.int32, (32, R), 0) + pi * OWN
    ownsel[...] = (lax.broadcasted_iota(jnp.int32, (32, R), 1) == own_rows).astype(F32)

    arrived(X_TEACH, "proto", teach)
    for p in range(NPR):
        v = teach[p]
        x32[4 * p : 4 * p + 4, 0:128] = v[0:4]
        x32[4 * p : 4 * p + 4, 128:256] = v[4:8]
    tgrp[dp] = x32[0:T, :].astype(BF16)

    def assign(g):
        rows = tgrp[g]
        for j in range(C // CH):
            e = jnp.exp(dot(rows, tpb[:, CH * j : CH * j + CH]) * TEACHER_SCALE)
            ass[group_rows(g), CH * j : CH * j + CH] = e
            assb[group_rows(g), CH * j : CH * j + CH] = e.astype(BF16)

    assign(dp)

    def column_part(g, acc, arow):
        if arow is not None:
            wide = row_to_columns(arow)
        for i in range(T // 8):
            e = ass[pl.ds(pl.multiple_of(g * T + 8 * i, 8), 8), :]
            if arow is not None:
                e = e * jnp.concatenate([wide[8 * i : 8 * i + 8]] * (C // 128), axis=1)
            acc = acc + e
        return acc

    def row_part(g):
        cb = jnp.broadcast_to(cvec[...], (8, C))
        parts = []
        for i in range(T // 8):
            parts.append(lane_tiles(ass[pl.ds(pl.multiple_of(g * T + 8 * i, 8), 8), :] * cb))
        return columns_to_row(jnp.concatenate(parts, axis=0))

    col1[dp] = jnp.sum(column_part(dp, jnp.zeros((8, C), F32), None), axis=0, keepdims=True)
    send(X_COL1, "dp", col1)
    send(X_TGRP, "dp", tgrp)
    arrived(X_STUDZ, "z", stud.at[py])
    send(X_STUDY, "y", stud)

    arrived(X_COL1, "dp", col1)
    cvec[...] = 1.0 / jnp.sum(col1[...], axis=0)
    row1[pi] = row_part(dp)
    send(X_ROW1, "proto", row1)

    arrived(X_STUDY, "y", stud)
    for p in range(NPR):
        v = stud[p % 4, p // 4].astype(F32)
        x32[OWN * p : OWN * p + OWN, 0:128] = v[0:OWN]
        x32[OWN * p : OWN * p + OWN, 128:256] = v[24 : 24 + OWN]
    xb[...] = x32[...].astype(BF16)
    for i in range(R // 128):
        xt[:, 128 * i : 128 * i + 128] = jnp.transpose(x32[128 * i : 128 * i + 128, :]).astype(BF16)

    @pl.loop(0, R // 128)
    def _(i):
        rows = pl.ds(pl.multiple_of(i * 128, 128), 128)
        part = jnp.zeros((128, 128), F32)
        for j in range(C // CH):
            e = jnp.exp(dot(xb[rows, :], wb[:, CH * j : CH * j + CH]) * STUDENT_SCALE)
            expo[rows, CH * j : CH * j + CH] = e
            expb[rows, CH * j : CH * j + CH] = e.astype(BF16)
            part = part + lane_tiles(e)
        tot[pi, pl.ds(i, 1), :] = columns_to_row(part)

    tot[pi, 5:8, :] = jnp.ones((3, 128), F32)

    arrived(X_ROW1, "proto", row1)
    avec[0:1, :] = 1.0 / jnp.sum(row1[...], axis=0)
    col2[dp] = jnp.sum(column_part(dp, jnp.zeros((8, C), F32), avec[0:1, :]), axis=0, keepdims=True)
    send(X_COL2, "dp", col2)
    send(X_TOT, "proto", tot)

    @pl.loop(0, R // 128)
    def _(i):
        rows = pl.ds(pl.multiple_of(i * 128, 128), 128)
        harr[rows, :] = dot_nt(expb[rows, :], wb[...])

    for p in range(NPR):
        hsend[p % 4, p // 4, 0:OWN, :] = harr[OWN * p : OWN * p + OWN, 0:128]
        hsend[p % 4, p // 4, OWN:HPAD, :] = harr[OWN * p : OWN * p + OWN, 128:256]
    send(X_HY, "y", hybuf, hsend)
    hybuf[py] = hsend[py]

    arrived(X_TGRP, "dp", tgrp)

    @pl.loop(1, NDP)
    def _(i):
        assign(lax.rem(dp + i, NDP))

    def columns():
        acc = lax.fori_loop(
            0, NDP, lambda g, acc: column_part(g, acc, avec[pl.ds(g, 1), :]), jnp.zeros((8, C), F32)
        )
        cvec[...] = 1.0 / jnp.sum(acc, axis=0, keepdims=True)

    def rows_into(buf):
        @pl.loop(0, NDP)
        def _(g):
            buf[pi, pl.ds(g, 1), :] = row_part(g)

    arrived(X_COL2, "dp", col2)
    cvec[...] = 1.0 / jnp.sum(col2[...], axis=0)
    rows_into(row2)
    send(X_ROW2, "proto", row2)

    arrived(X_HY, "y", hybuf)
    for z in range(8):
        hzsend[z] = jnp.sum(hybuf[:, z], axis=0)
    send(X_HZ, "z", hzbuf, hzsend)
    hzbuf[pz] = hzsend[pz]

    ut = dot(xt[...], selb[...])
    for g in range(NDP):
        utsend[g] = ut[32 * g : 32 * g + 32, :]
    send(X_UT, "dp", utbuf, utsend)
    utbuf[dp] = utsend[dp]

    arrived(X_TOT, "proto", tot)
    inv_tot = 1.0 / jnp.sum(tot[...], axis=0)
    for i in range(R // 128):
        rows = slice(128 * i, 128 * i + 128)
        scalec[rows, :] = scalec[rows, :] * row_to_columns(inv_tot[i : i + 1, :])

    @pl.loop(0, R // 16)
    def _(i):
        rows = pl.ds(pl.multiple_of(i * 16, 16), 16)
        s = scalec[rows, :]
        probb[rows, :] = (expo[rows, :] * jnp.concatenate([s] * (C // 128), axis=1)).astype(BF16)

    for j in range(C // CH):
        cols = slice(CH * j, CH * j + CH)
        pg = dot(xt[...], probb[:, cols])
        direction = pr[:, cols].astype(F32) / pnorm[:, cols]
        pg = (pg - direction * jnp.sum(direction * pg, axis=0, keepdims=True)).astype(BF16)
        for g in range(NDP):
            pgsend[g, :, cols] = pg[32 * g : 32 * g + 32, :]
    send(X_PG, "dp", pgbuf, pgsend)
    pgbuf[dp] = pgsend[dp]

    arrived(X_ROW2, "proto", row2)
    avec[...] = 1.0 / jnp.sum(row2[...], axis=0)
    columns()

    cb = jnp.broadcast_to(cvec[...], (16, C))
    for i in range(T // 16):
        rows = pl.ds(pl.multiple_of(dp * T + 16 * i, 16), 16)
        probb[16 * i : 16 * i + 16, :] = (ass[rows, :] * cb).astype(BF16)
    garr[...] = dot_nt(probb[0:T, :], wb[...])
    for p in range(16):
        gsend[p] = garr[8 * p : 8 * p + 8, 0:128]
        gsend[p + 16] = garr[8 * p : 8 * p + 8, 128:256]
    send(X_G, "proto", gbuf, gsend)
    gbuf[pi] = gsend[pi]
    rows_into(row3)
    send(X_ROW3, "proto", row3)

    arrived(X_HZ, "z", hzbuf)
    hsum = jnp.sum(hzbuf[...], axis=0)
    own_scale = jnp.dot(ownsel[...], scalec[...], precision=lax.Precision.HIGHEST, preferred_element_type=F32)[0:OWN, 0:1]
    own_pick = dot(ownsel[...].astype(BF16), selb[...])[0:OWN, :]

    arrived(X_G, "proto", gbuf)
    gall[pi] = jnp.sum(gbuf[...], axis=0)
    send(X_GALL, "proto", gall)

    arrived(X_ROW3, "proto", row3)
    avec[...] = 1.0 / jnp.sum(row3[...], axis=0)
    arrived(X_UT, "dp", utbuf)
    lhs = jnp.concatenate([utbuf[g] * avec[g : g + 1, :] for g in range(NDP)], axis=1)
    high = lhs.astype(BF16)
    lhs = jnp.concatenate([high, (lhs - high.astype(F32)).astype(BF16)], axis=0)
    arrived(X_PG, "dp", pgbuf)
    own32 = pl.ds(pl.multiple_of(dp * 32, 32), 32)
    for j in range(C // CH):
        cols = slice(CH * j, CH * j + CH)
        both = dot(lhs, assb[:, cols])
        target = (both[0:32] + both[32:64]) * cvec[:, cols]
        own = GRAD_SCALE * (jnp.sum(pgbuf[:, :, cols].astype(F32), axis=0) - target)
        own_dir = pr[own32, cols].astype(F32) / pnorm[:, cols]
        pown[:, cols] = own
        pdir[:, cols] = own_dir
        dotbuf[dp, :, cols] = jnp.sum(own * own_dir, axis=0, keepdims=True)
    send(X_DOT, "dp", dotbuf)

    arrived(X_GALL, "proto", gall)
    gfull = jnp.concatenate([gall[0:16].reshape(T, 128), gall[16:32].reshape(T, 128)], axis=1)
    picked = jnp.dot(
        own_pick * avec[pl.ds(dp, 1), :], gfull, precision=lax.Precision.HIGHEST, preferred_element_type=F32
    )
    h = jnp.concatenate([hsum[0:OWN], hsum[OWN:HPAD]], axis=1)
    unit_grad = GRAD_SCALE * (own_scale * h - picked)
    sd = sdir[...]
    sgrad[...] = (unit_grad - sd * jnp.sum(sd * unit_grad, axis=1, keepdims=True)) / snorm[:, 0:1]

    arrived(X_DOT, "dp", dotbuf)
    pdot[...] = jnp.sum(dotbuf[...], axis=0)

    for x, axis, buf in (
        (X_TEACH, "proto", teach), (X_STUDZ, "z", stud.at[py]), (X_STUDY, "y", stud), (X_COL1, "dp", col1),
        (X_TGRP, "dp", tgrp), (X_ROW1, "proto", row1), (X_COL2, "dp", col2), (X_TOT, "proto", tot),
        (X_ROW2, "proto", row2), (X_HY, "y", hybuf), (X_HZ, "z", hzbuf), (X_UT, "dp", utbuf), (X_ROW3, "proto", row3),
        (X_G, "proto", gbuf), (X_PG, "dp", pgbuf), (X_GALL, "proto", gall), (X_DOT, "dp", dotbuf),
    ):
        sent(x, axis, buf)


def last_step(unit_grad, own, own_dir, column_dot, norm, sgrad, pgrad):
    sgrad[...] = unit_grad[...]
    pgrad[...] = (own[...] - own_dir[...] * column_dot[...]) / norm[...]


def per_device(student_feats, teacher_feats, prototypes, teacher_prototypes, crop_image, pairing):
    vmem = pl.BlockSpec(memory_space=pltpu.VMEM)
    unit_grad, own, own_dir, column_dot, norm = pl.pallas_call(
        kernel,
        out_shape=(
            jax.ShapeDtypeStruct((OWN, K), F32),
            jax.ShapeDtypeStruct((K // NDP, C), F32),
            jax.ShapeDtypeStruct((K // NDP, C), F32),
            jax.ShapeDtypeStruct((1, C), F32),
            jax.ShapeDtypeStruct((1, C), F32),
        ),
        in_specs=[pl.BlockSpec(memory_space=pl.ANY)] * 6,
        out_specs=(vmem,) * 5,
        scratch_shapes=[
            pltpu.VMEM((NPR, 8, 128), F32),
            pltpu.VMEM((4, 8, PAD, 128), BF16),
            pltpu.VMEM((NDP, 1, C), F32),
            pltpu.VMEM((NDP, T, K), BF16),
            pltpu.VMEM((NPR, 1, 128), F32),
            pltpu.VMEM((NDP, 1, C), F32),
            pltpu.VMEM((NPR, 8, 128), F32),
            pltpu.VMEM((NPR, 8, 128), F32),
            pltpu.VMEM((4, 8, HPAD, 128), F32),
            pltpu.VMEM((8, HPAD, 128), F32),
            pltpu.VMEM((NDP, 32, 128), F32),
            pltpu.VMEM((NPR, 8, 128), F32),
            pltpu.VMEM((NPR, 8, 128), F32),
            pltpu.VMEM((NDP, 32, C), BF16),
            pltpu.VMEM((NPR, 8, 128), F32),
            pltpu.VMEM((NDP, 1, C), F32),
            pltpu.VMEM((4, 8, HPAD, 128), F32),
            pltpu.VMEM((8, HPAD, 128), F32),
            pltpu.VMEM((NDP, 32, 128), F32),
            pltpu.VMEM((NPR, 8, 128), F32),
            pltpu.VMEM((NDP, 32, C), BF16),
            pltpu.VMEM((PAD, 128), F32),
            pltpu.VMEM((R, K), F32),
            pltpu.VMEM((R, K), BF16),
            pltpu.VMEM((K, R), BF16),
            pltpu.VMEM((K, C), BF16),
            pltpu.VMEM((K, C), BF16),
            pltpu.VMEM((R, C), F32),
            pltpu.VMEM((R, C), BF16),
            pltpu.VMEM((R, C), BF16),
            pltpu.VMEM((R, 128), BF16),
            pltpu.VMEM((R, 128), F32),
            pltpu.VMEM((R, K), F32),
            pltpu.VMEM((T, K), F32),
            pltpu.VMEM((NDP * T, C), F32),
            pltpu.VMEM((NDP * T, C), BF16),
            pltpu.VMEM((1, C), F32),
            pltpu.VMEM((8, 128), F32),
            pltpu.VMEM((OWN, K), F32),
            pltpu.VMEM((OWN, 128), F32),
            pltpu.VMEM((32, R), F32),
            pltpu.VMEM((OWN, K), BF16),
            pltpu.VMEM((4, K), BF16),
            pltpu.VMEM((K, C), BF16),
            pltpu.VMEM((K, C), BF16),
            pltpu.VMEM((R // 128, 128), jnp.int32),
            pltpu.VMEM((2, R), jnp.int32),
            pltpu.SemaphoreType.DMA((N_X,)),
            pltpu.SemaphoreType.DMA((N_X,)),
            pltpu.SemaphoreType.DMA((6,)),
        ],
        compiler_params=pltpu.CompilerParams(
            collective_id=0, has_side_effects=True, vmem_limit_bytes=56 * 2**20
        ),
    )(student_feats, teacher_feats, prototypes, teacher_prototypes, crop_image.reshape(R // 128, 128), pairing.T)
    return pl.pallas_call(
        last_step,
        out_shape=(jax.ShapeDtypeStruct((OWN, K), F32), jax.ShapeDtypeStruct((K // NDP, C), F32)),
        in_specs=[vmem] * 5,
        out_specs=(vmem, vmem),
    )(unit_grad, own, own_dir, column_dot, norm)


def solution(mesh):
    in_specs = (
        P(("dp", "proto"), None),
        P(("dp", "proto"), None),
        P(None, "proto"),
        P(None, "proto"),
        P("dp"),
        P("dp", None),
    )
    out_specs = (P(("dp", "proto"), None), P("dp", "proto"))
    return jax.shard_map(
        per_device, mesh=mesh, in_specs=in_specs, out_specs=out_specs, check_vma=False
    )
```

```python
import jax
import jax.numpy as jnp
from jax import lax
from jax.experimental import pallas as pl
from jax.experimental.pallas import tpu as pltpu
from jax.sharding import PartitionSpec as P

MESH = pl.DeviceIdType.MESH
F32 = jnp.float32
BF16 = jnp.bfloat16

IMG_DEV = 64
EPS = 1e-06
TEACHER_SCALE = 1.0 / 0.07
STUDENT_SCALE = 1.0 / 0.1
GRAD_SCALE = 4096.0 / 0.1

NDP = 8
NPR = 32
K = 256
C = 2048
R = 640
T = 128
OWN = 20
PAD = 48
HPAD = 40
CH = 512

(
    X_TEACH, X_STUDZ, X_STUDY, X_COL1, X_TGRP, X_ROW1, X_COL2, X_TOT, X_ROW2, X_HY, X_HZ, X_UT, X_ROW3, X_G, X_PG, X_GALL, X_DOT
) = range(17)
N_X = 17
SIZES = {"dp": 8, "proto": 32, "z": 8, "y": 4}


def row_to_columns(row):
    return jnp.transpose(jnp.broadcast_to(row, (128, 128)))


def columns_to_row(part):
    return jnp.sum(jnp.transpose(part), axis=0, keepdims=True)


def lane_tiles(value):
    total = value[:, 0:128]
    for j in range(1, value.shape[1] // 128):
        total = total + value[:, 128 * j : 128 * j + 128]
    return total


def dot(a, b):
    return jnp.dot(a, b, preferred_element_type=F32)


def dot_nt(a, b):
    return lax.dot_general(a, b, (((1,), (1,)), ((), ())), preferred_element_type=F32)


def kernel(
    sfh, tfh, prh, tph, croph, pairh,
    sgrad, pown, pdir, pdot, pnorm,
    teach, stud, col1, tgrp, row1, col2, tot, row2, hybuf, hzbuf, utbuf, row3, gbuf, pgbuf, gall, dotbuf,
    hsend, hzsend, utsend, gsend, pgsend,
    pack, x32, xb, xt, wb, tpb, expo, expb, probb, selb, scalec, harr, garr, ass, assb, mown, cvec, avec,
    sdir, snorm, ownsel, sf, tf, pr, tp, crop, pair,
    ssem, rsem, lsem,
):
    dp = lax.axis_index("dp")
    pi = lax.axis_index("proto")

    pz, py = pi // 4, lax.rem(pi, 4)

    def far_first(i, half):
        return half + ((i + 1) // 2) * (1 - 2 * lax.rem(i, 2))

    def peer(axis, i):
        if axis == "dp":
            return lax.rem(dp + i + 1, NDP)
        if axis == "z":
            return lax.rem(pz + far_first(i, 4), 8)
        if axis == "y":
            return lax.rem(py + far_first(i, 2), 4)
        return lax.rem(pz + far_first(i // 4, 4), 8) * 4 + lax.rem(py + far_first(lax.rem(i, 4), 2), 4)

    def address(axis, p):
        if axis == "dp":
            return (p, pi)
        if axis == "z":
            return (dp, p * 4 + py)
        if axis == "y":
            return (dp, pz * 4 + p)
        return (dp, p)

    def mine(axis):
        return {"dp": dp, "proto": pi, "z": pz, "y": py}[axis]

    def count(axis):
        return SIZES[axis]

    def send(x, axis, dst, src=None):
        me = mine(axis)

        @pl.loop(0, count(axis) - 1)
        def _(i):
            p = peer(axis, i)
            pltpu.make_async_remote_copy(
                src_ref=dst.at[me] if src is None else src.at[p],
                dst_ref=dst.at[me],
                send_sem=ssem.at[x],
                recv_sem=rsem.at[x],
                device_id=address(axis, p),
                device_id_type=MESH,
            ).start()

    def arrived(x, axis, dst):
        blocks = dst.at[pl.ds(0, count(axis) - 1)]
        pltpu.make_async_copy(blocks, blocks, rsem.at[x]).wait()

    def sent(x, axis, dst):
        blocks = dst.at[pl.ds(0, count(axis) - 1)]
        pltpu.make_async_copy(blocks, blocks, ssem.at[x]).wait()

    def group_rows(g):
        return pl.ds(pl.multiple_of(g * T, T), T)

    barrier = pltpu.get_barrier_semaphore()
    for axis in ("proto", "dp"):
        @pl.loop(0, count(axis) - 1)
        def _(i, axis=axis):
            p = peer(axis, i)
            pl.semaphore_signal(barrier, inc=1, device_id=address(axis, p), device_id_type=MESH)

    loads = []
    for k, (src, dst) in enumerate(
        ((tfh, tf), (sfh, sf), (tph, tp), (prh, pr), (croph, crop), (pairh, pair))
    ):
        loads.append(pltpu.make_async_copy(src, dst, lsem.at[k]))
        loads[-1].start()

    loads[0].wait()
    tw = tf[...].astype(F32)
    tu = tw / jnp.sqrt(jnp.sum(tw * tw, axis=1, keepdims=True) + EPS)
    teach[pi, 0:4, :] = tu[:, 0:128].astype(BF16).astype(F32)
    teach[pi, 4:8, :] = tu[:, 128:256].astype(BF16).astype(F32)
    loads[1].wait()
    sw = sf[...].astype(F32)
    sn = jnp.sqrt(jnp.sum(sw * sw, axis=1, keepdims=True) + EPS)
    sd = sw / sn
    snorm[...] = jnp.broadcast_to(sn, (OWN, 128))
    sdir[...] = sd
    pack[...] = jnp.zeros_like(pack)
    pack[0:OWN, :] = sd[:, 0:128]
    pack[24 : 24 + OWN, :] = sd[:, 128:256]
    stud[py, pz] = pack[...].astype(BF16)

    loads[2].wait()

    @pl.loop(0, C // 256)
    def _(j):
        cols = pl.ds(pl.multiple_of(j * 256, 256), 256)
        v = tp[:, cols].astype(F32)
        inv = 1.0 / jnp.sqrt(jnp.sum(v * v, axis=0, keepdims=True) + EPS)
        tpb[:, cols] = (v * inv).astype(BF16)

    pl.semaphore_wait(barrier, NPR - 1 + NDP - 1)
    send(X_TEACH, "proto", teach)
    send(X_STUDZ, "z", stud.at[py])

    loads[3].wait()

    @pl.loop(0, C // 256)
    def _(j):
        cols = pl.ds(pl.multiple_of(j * 256, 256), 256)
        v = pr[:, cols].astype(F32)
        n = jnp.sqrt(jnp.sum(v * v, axis=0, keepdims=True) + EPS)
        pnorm[:, cols] = n
        wb[:, cols] = (v * (1.0 / n)).astype(BF16)

    loads[4].wait()
    loads[5].wait()
    lanes = lax.broadcasted_iota(jnp.int32, (128, 128), 1).astype(F32)
    base = (dp * IMG_DEV).astype(F32)
    for i in range(R // 128):
        image = row_to_columns(crop[i : i + 1, :].astype(F32)) - base
        w0 = row_to_columns(pair[0:1, 128 * i : 128 * i + 128].astype(F32))
        w1 = row_to_columns(pair[1:2, 128 * i : 128 * i + 128].astype(F32))
        sel = jnp.where(lanes == 2.0 * image, w0, 0.0) + jnp.where(lanes == 2.0 * image + 1.0, w1, 0.0)
        selb[128 * i : 128 * i + 128, :] = sel.astype(BF16)
        scalec[128 * i : 128 * i + 128, :] = w0 + w1
    own_rows = lax.broadcasted_iota(jnp.int32, (32, R), 0) + pi * OWN
    ownsel[...] = (lax.broadcasted_iota(jnp.int32, (32, R), 1) == own_rows).astype(F32)

    arrived(X_TEACH, "proto", teach)
    for p in range(NPR):
        v = teach[p]
        x32[4 * p : 4 * p + 4, 0:128] = v[0:4]
        x32[4 * p : 4 * p + 4, 128:256] = v[4:8]
    tgrp[dp] = x32[0:T, :].astype(BF16)

    def assign(g):
        rows = tgrp[g]
        for j in range(C // CH):
            e = jnp.exp(dot(rows, tpb[:, CH * j : CH * j + CH]) * TEACHER_SCALE)
            ass[group_rows(g), CH * j : CH * j + CH] = e
            assb[group_rows(g), CH * j : CH * j + CH] = e.astype(BF16)

    assign(dp)

    def column_part(g, acc, arow, table=ass):
        if arow is not None:
            wide = row_to_columns(arow)
        for i in range(T // 8):
            e = table[pl.ds(pl.multiple_of(g * T + 8 * i, 8), 8), :]
            if arow is not None:
                e = e * jnp.concatenate([wide[8 * i : 8 * i + 8]] * (C // 128), axis=1)
            acc = acc + e
        return acc

    def row_part(g):
        cb = jnp.broadcast_to(cvec[...], (8, C))
        parts = []
        for i in range(T // 8):
            parts.append(lane_tiles(ass[pl.ds(pl.multiple_of(g * T + 8 * i, 8), 8), :] * cb))
        return columns_to_row(jnp.concatenate(parts, axis=0))

    col1[dp] = jnp.sum(column_part(dp, jnp.zeros((8, C), F32), None), axis=0, keepdims=True)
    send(X_COL1, "dp", col1)
    send(X_TGRP, "dp", tgrp)
    arrived(X_STUDZ, "z", stud.at[py])
    send(X_STUDY, "y", stud)

    arrived(X_COL1, "dp", col1)
    cvec[...] = 1.0 / jnp.sum(col1[...], axis=0)
    row1[pi] = row_part(dp)
    send(X_ROW1, "proto", row1)

    arrived(X_STUDY, "y", stud)
    for p in range(NPR):
        v = stud[p % 4, p // 4].astype(F32)
        x32[OWN * p : OWN * p + OWN, 0:128] = v[0:OWN]
        x32[OWN * p : OWN * p + OWN, 128:256] = v[24 : 24 + OWN]
    xb[...] = x32[...].astype(BF16)
    for i in range(R // 128):
        xt[:, 128 * i : 128 * i + 128] = jnp.transpose(x32[128 * i : 128 * i + 128, :]).astype(BF16)

    @pl.loop(0, R // 128)
    def _(i):
        rows = pl.ds(pl.multiple_of(i * 128, 128), 128)
        part = jnp.zeros((128, 128), F32)
        for j in range(C // CH):
            e = jnp.exp(dot(xb[rows, :], wb[:, CH * j : CH * j + CH]) * STUDENT_SCALE)
            expo[rows, CH * j : CH * j + CH] = e
            expb[rows, CH * j : CH * j + CH] = e.astype(BF16)
            part = part + lane_tiles(e)
        tot[pi, pl.ds(i, 1), :] = columns_to_row(part)

    tot[pi, 5:8, :] = jnp.ones((3, 128), F32)

    arrived(X_ROW1, "proto", row1)
    avec[0:1, :] = 1.0 / jnp.sum(row1[...], axis=0)
    col2[dp] = jnp.sum(column_part(dp, jnp.zeros((8, C), F32), avec[0:1, :]), axis=0, keepdims=True)
    send(X_COL2, "dp", col2)
    send(X_TOT, "proto", tot)

    @pl.loop(0, R // 128)
    def _(i):
        rows = pl.ds(pl.multiple_of(i * 128, 128), 128)
        harr[rows, :] = dot_nt(expb[rows, :], wb[...])

    for p in range(NPR):
        hsend[p % 4, p // 4, 0:OWN, :] = harr[OWN * p : OWN * p + OWN, 0:128]
        hsend[p % 4, p // 4, OWN:HPAD, :] = harr[OWN * p : OWN * p + OWN, 128:256]
    hybuf[py] = hsend[py]

    arrived(X_TGRP, "dp", tgrp)

    @pl.loop(1, NDP)
    def _(i):
        assign(lax.rem(dp + i, NDP))

    def columns():
        acc = lax.fori_loop(
            0, NDP, lambda g, acc: column_part(g, acc, avec[pl.ds(g, 1), :]), jnp.zeros((8, C), F32)
        )
        cvec[...] = 1.0 / jnp.sum(acc, axis=0, keepdims=True)

    def rows_into(buf):
        @pl.loop(0, NDP)
        def _(g):
            buf[pi, pl.ds(g, 1), :] = row_part(g)

    arrived(X_COL2, "dp", col2)
    cvec[...] = 1.0 / jnp.sum(col2[...], axis=0)
    rows_into(row2)
    send(X_ROW2, "proto", row2)
    send(X_HY, "y", hybuf, hsend)

    ut = dot(xt[...], selb[...])
    for g in range(NDP):
        utsend[g] = ut[32 * g : 32 * g + 32, :]
    send(X_UT, "dp", utbuf, utsend)
    utbuf[dp] = utsend[dp]

    arrived(X_TOT, "proto", tot)
    inv_tot = 1.0 / jnp.sum(tot[...], axis=0)
    for i in range(R // 128):
        rows = slice(128 * i, 128 * i + 128)
        scalec[rows, :] = scalec[rows, :] * row_to_columns(inv_tot[i : i + 1, :])

    @pl.loop(0, R // 16)
    def _(i):
        rows = pl.ds(pl.multiple_of(i * 16, 16), 16)
        s = scalec[rows, :]
        probb[rows, :] = (expo[rows, :] * jnp.concatenate([s] * (C // 128), axis=1)).astype(BF16)

    for j in range(C // CH):
        cols = slice(CH * j, CH * j + CH)
        pg = dot(xt[...], probb[:, cols])
        direction = pr[:, cols].astype(F32) / pnorm[:, cols]
        pg = (pg - direction * jnp.sum(direction * pg, axis=0, keepdims=True)).astype(BF16)
        for g in range(NDP):
            pgsend[g, :, cols] = pg[32 * g : 32 * g + 32, :]
    send(X_PG, "dp", pgbuf, pgsend)
    pgbuf[dp] = pgsend[dp]

    utb = ut.astype(BF16)
    for j in range(C // CH):
        cols = slice(CH * j, CH * j + CH)
        along = lax.dot_general(utb, wb[:, cols], (((0,), (0,)), ((), ())), preferred_element_type=F32)
        mown[:, cols] = along * ass[group_rows(dp), cols]

    arrived(X_ROW2, "proto", row2)
    avec[...] = 1.0 / jnp.sum(row2[...], axis=0)
    columns()

    cb = jnp.broadcast_to(cvec[...], (16, C))
    for i in range(T // 16):
        rows = pl.ds(pl.multiple_of(dp * T + 16 * i, 16), 16)
        probb[16 * i : 16 * i + 16, :] = (ass[rows, :] * cb).astype(BF16)
    garr[...] = dot_nt(probb[0:T, :], wb[...])
    for p in range(16):
        gsend[p] = garr[8 * p : 8 * p + 8, 0:128]
        gsend[p + 16] = garr[8 * p : 8 * p + 8, 128:256]
    send(X_G, "proto", gbuf, gsend)
    gbuf[pi] = gsend[pi]
    rows_into(row3)
    send(X_ROW3, "proto", row3)

    arrived(X_HY, "y", hybuf)
    for z in range(8):
        hzsend[z] = jnp.sum(hybuf[:, z], axis=0)
    send(X_HZ, "z", hzbuf, hzsend)
    hzbuf[pz] = hzsend[pz]

    arrived(X_HZ, "z", hzbuf)
    hsum = jnp.sum(hzbuf[...], axis=0)
    own_scale = jnp.dot(ownsel[...], scalec[...], precision=lax.Precision.HIGHEST, preferred_element_type=F32)[0:OWN, 0:1]
    own_pick = dot(ownsel[...].astype(BF16), selb[...])[0:OWN, :]

    arrived(X_G, "proto", gbuf)
    gall[pi] = jnp.sum(gbuf[...], axis=0)
    send(X_GALL, "proto", gall)

    arrived(X_ROW3, "proto", row3)
    avec[...] = 1.0 / jnp.sum(row3[...], axis=0)
    along = jnp.sum(column_part(0, jnp.zeros((8, C), F32), avec[pl.ds(dp, 1), :], mown), axis=0, keepdims=True)
    dotbuf[dp] = along * cvec[...]
    send(X_DOT, "dp", dotbuf)
    arrived(X_UT, "dp", utbuf)
    lhs = jnp.concatenate([utbuf[g] * avec[g : g + 1, :] for g in range(NDP)], axis=1)
    high = lhs.astype(BF16)
    lhs = jnp.concatenate([high, (lhs - high.astype(F32)).astype(BF16)], axis=0)
    arrived(X_PG, "dp", pgbuf)
    own32 = pl.ds(pl.multiple_of(dp * 32, 32), 32)
    for j in range(C // CH):
        cols = slice(CH * j, CH * j + CH)
        both = dot(lhs, assb[:, cols])
        target = (both[0:32] + both[32:64]) * cvec[:, cols]
        own = GRAD_SCALE * (jnp.sum(pgbuf[:, :, cols].astype(F32), axis=0) - target)
        own_dir = pr[own32, cols].astype(F32) / pnorm[:, cols]
        pown[:, cols] = own
        pdir[:, cols] = own_dir

    arrived(X_GALL, "proto", gall)
    gfull = jnp.concatenate([gall[0:16].reshape(T, 128), gall[16:32].reshape(T, 128)], axis=1)
    picked = jnp.dot(
        own_pick * avec[pl.ds(dp, 1), :], gfull, precision=lax.Precision.HIGHEST, preferred_element_type=F32
    )
    h = jnp.concatenate([hsum[0:OWN], hsum[OWN:HPAD]], axis=1)
    unit_grad = GRAD_SCALE * (own_scale * h - picked)
    sd = sdir[...]
    sgrad[...] = (unit_grad - sd * jnp.sum(sd * unit_grad, axis=1, keepdims=True)) / snorm[:, 0:1]

    arrived(X_DOT, "dp", dotbuf)
    pdot[...] = -GRAD_SCALE * jnp.sum(dotbuf[...], axis=0)

    for x, axis, buf in (
        (X_TEACH, "proto", teach), (X_STUDZ, "z", stud.at[py]), (X_STUDY, "y", stud), (X_COL1, "dp", col1),
        (X_TGRP, "dp", tgrp), (X_ROW1, "proto", row1), (X_COL2, "dp", col2), (X_TOT, "proto", tot),
        (X_ROW2, "proto", row2), (X_HY, "y", hybuf), (X_HZ, "z", hzbuf), (X_UT, "dp", utbuf), (X_ROW3, "proto", row3),
        (X_G, "proto", gbuf), (X_PG, "dp", pgbuf), (X_GALL, "proto", gall), (X_DOT, "dp", dotbuf),
    ):
        sent(x, axis, buf)


def last_step(unit_grad, own, own_dir, column_dot, norm, sgrad, pgrad):
    sgrad[...] = unit_grad[...]
    pgrad[...] = (own[...] - own_dir[...] * column_dot[...]) / norm[...]


def per_device(student_feats, teacher_feats, prototypes, teacher_prototypes, crop_image, pairing):
    vmem = pl.BlockSpec(memory_space=pltpu.VMEM)
    unit_grad, own, own_dir, column_dot, norm = pl.pallas_call(
        kernel,
        out_shape=(
            jax.ShapeDtypeStruct((OWN, K), F32),
            jax.ShapeDtypeStruct((K // NDP, C), F32),
            jax.ShapeDtypeStruct((K // NDP, C), F32),
            jax.ShapeDtypeStruct((1, C), F32),
            jax.ShapeDtypeStruct((1, C), F32),
        ),
        in_specs=[pl.BlockSpec(memory_space=pl.ANY)] * 6,
        out_specs=(vmem,) * 5,
        scratch_shapes=[
            pltpu.VMEM((NPR, 8, 128), F32),
            pltpu.VMEM((4, 8, PAD, 128), BF16),
            pltpu.VMEM((NDP, 1, C), F32),
            pltpu.VMEM((NDP, T, K), BF16),
            pltpu.VMEM((NPR, 1, 128), F32),
            pltpu.VMEM((NDP, 1, C), F32),
            pltpu.VMEM((NPR, 8, 128), F32),
            pltpu.VMEM((NPR, 8, 128), F32),
            pltpu.VMEM((4, 8, HPAD, 128), F32),
            pltpu.VMEM((8, HPAD, 128), F32),
            pltpu.VMEM((NDP, 32, 128), F32),
            pltpu.VMEM((NPR, 8, 128), F32),
            pltpu.VMEM((NPR, 8, 128), F32),
            pltpu.VMEM((NDP, 32, C), BF16),
            pltpu.VMEM((NPR, 8, 128), F32),
            pltpu.VMEM((NDP, 1, C), F32),
            pltpu.VMEM((4, 8, HPAD, 128), F32),
            pltpu.VMEM((8, HPAD, 128), F32),
            pltpu.VMEM((NDP, 32, 128), F32),
            pltpu.VMEM((NPR, 8, 128), F32),
            pltpu.VMEM((NDP, 32, C), BF16),
            pltpu.VMEM((PAD, 128), F32),
            pltpu.VMEM((R, K), F32),
            pltpu.VMEM((R, K), BF16),
            pltpu.VMEM((K, R), BF16),
            pltpu.VMEM((K, C), BF16),
            pltpu.VMEM((K, C), BF16),
            pltpu.VMEM((R, C), F32),
            pltpu.VMEM((R, C), BF16),
            pltpu.VMEM((R, C), BF16),
            pltpu.VMEM((R, 128), BF16),
            pltpu.VMEM((R, 128), F32),
            pltpu.VMEM((R, K), F32),
            pltpu.VMEM((T, K), F32),
            pltpu.VMEM((NDP * T, C), F32),
            pltpu.VMEM((NDP * T, C), BF16),
            pltpu.VMEM((T, C), F32),
            pltpu.VMEM((1, C), F32),
            pltpu.VMEM((8, 128), F32),
            pltpu.VMEM((OWN, K), F32),
            pltpu.VMEM((OWN, 128), F32),
            pltpu.VMEM((32, R), F32),
            pltpu.VMEM((OWN, K), BF16),
            pltpu.VMEM((4, K), BF16),
            pltpu.VMEM((K, C), BF16),
            pltpu.VMEM((K, C), BF16),
            pltpu.VMEM((R // 128, 128), jnp.int32),
            pltpu.VMEM((2, R), jnp.int32),
            pltpu.SemaphoreType.DMA((N_X,)),
            pltpu.SemaphoreType.DMA((N_X,)),
            pltpu.SemaphoreType.DMA((6,)),
        ],
        compiler_params=pltpu.CompilerParams(
            collective_id=0, has_side_effects=True, vmem_limit_bytes=56 * 2**20
        ),
    )(student_feats, teacher_feats, prototypes, teacher_prototypes, crop_image.reshape(R // 128, 128), pairing.T)
    return pl.pallas_call(
        last_step,
        out_shape=(jax.ShapeDtypeStruct((OWN, K), F32), jax.ShapeDtypeStruct((K // NDP, C), F32)),
        in_specs=[vmem] * 5,
        out_specs=(vmem, vmem),
    )(unit_grad, own, own_dir, column_dot, norm)


def solution(mesh):
    in_specs = (
        P(("dp", "proto"), None),
        P(("dp", "proto"), None),
        P(None, "proto"),
        P(None, "proto"),
        P("dp"),
        P("dp", None),
    )
    out_specs = (P(("dp", "proto"), None), P("dp", "proto"))
    return jax.shard_map(
        per_device, mesh=mesh, in_specs=in_specs, out_specs=out_specs, check_vma=False
    )
```

```python
import jax
import jax.numpy as jnp
from jax import lax
from jax.experimental import pallas as pl
from jax.experimental.pallas import tpu as pltpu
from jax.sharding import PartitionSpec as P

MESH = pl.DeviceIdType.MESH
F32 = jnp.float32
BF16 = jnp.bfloat16

IMG_DEV = 64
EPS = 1e-06
TEACHER_SCALE = 1.0 / 0.07
STUDENT_SCALE = 1.0 / 0.1
GRAD_SCALE = 4096.0 / 0.1

NDP = 8
NPR = 32
K = 256
C = 2048
R = 640
T = 128
OWN = 20
PAD = 48
HPAD = 24
CH = 512

(
    X_TEACH, X_STUDZ, X_STUDY, X_COL1, X_TGRP, X_ROW1, X_COL2, X_TOT, X_ROW2, X_HY0, X_HY1, X_HZ0, X_HZ1, X_UT, X_ROW3, X_G, X_PG, X_GALL, X_DOT
) = range(19)
N_X = 19
SIZES = {"dp": 8, "proto": 32, "z": 8, "y": 4}


def row_to_columns(row):
    return jnp.transpose(jnp.broadcast_to(row, (128, 128)))


def columns_to_row(part):
    return jnp.sum(jnp.transpose(part), axis=0, keepdims=True)


def lane_tiles(value):
    total = value[:, 0:128]
    for j in range(1, value.shape[1] // 128):
        total = total + value[:, 128 * j : 128 * j + 128]
    return total


def dot(a, b):
    return jnp.dot(a, b, preferred_element_type=F32)


def dot_nt(a, b):
    return lax.dot_general(a, b, (((1,), (1,)), ((), ())), preferred_element_type=F32)


def kernel(
    sfh, tfh, prh, tph, croph, pairh,
    sgrad, pgrad,
    teach, stud, col1, tgrp, row1, col2, tot, row2, hybuf, hzbuf, utbuf, row3, gbuf, pgbuf, gall, dotbuf,
    hsend, hzsend, utsend, gsend, pgsend,
    pack, x32, xb, xt, wb, tpb, pnorm, pown, expo, expb, probb, selb, scalec, harr, garr, ass, assb, mown, cvec, avec,
    sdir, snorm, ownsel, sf, tf, pr, tp, crop, pair,
    ssem, rsem, lsem,
):
    dp = lax.axis_index("dp")
    pi = lax.axis_index("proto")

    pz, py = pi // 4, lax.rem(pi, 4)

    def far_first(i, half):
        return half + ((i + 1) // 2) * (1 - 2 * lax.rem(i, 2))

    def peer(axis, i):
        if axis == "dp":
            return lax.rem(dp + i + 1, NDP)
        if axis == "z":
            return lax.rem(pz + far_first(i, 4), 8)
        if axis == "y":
            return lax.rem(py + far_first(i, 2), 4)
        return lax.rem(pz + far_first(i // 4, 4), 8) * 4 + lax.rem(py + far_first(lax.rem(i, 4), 2), 4)

    def address(axis, p):
        if axis == "dp":
            return (p, pi)
        if axis == "z":
            return (dp, p * 4 + py)
        if axis == "y":
            return (dp, pz * 4 + p)
        return (dp, p)

    def mine(axis):
        return {"dp": dp, "proto": pi, "z": pz, "y": py}[axis]

    def count(axis):
        return SIZES[axis]

    def send(x, axis, dst, src=None):
        me = mine(axis)

        @pl.loop(0, count(axis) - 1)
        def _(i):
            p = peer(axis, i)
            pltpu.make_async_remote_copy(
                src_ref=dst.at[me] if src is None else src.at[p],
                dst_ref=dst.at[me],
                send_sem=ssem.at[x],
                recv_sem=rsem.at[x],
                device_id=address(axis, p),
                device_id_type=MESH,
            ).start()

    def arrived(x, axis, dst):
        blocks = dst.at[pl.ds(0, count(axis) - 1)]
        pltpu.make_async_copy(blocks, blocks, rsem.at[x]).wait()

    def sent(x, axis, dst):
        blocks = dst.at[pl.ds(0, count(axis) - 1)]
        pltpu.make_async_copy(blocks, blocks, ssem.at[x]).wait()

    def group_rows(g):
        return pl.ds(pl.multiple_of(g * T, T), T)

    barrier = pltpu.get_barrier_semaphore()
    for axis in ("proto", "dp"):
        @pl.loop(0, count(axis) - 1)
        def _(i, axis=axis):
            p = peer(axis, i)
            pl.semaphore_signal(barrier, inc=1, device_id=address(axis, p), device_id_type=MESH)

    loads = []
    for k, (src, dst) in enumerate(
        ((tfh, tf), (sfh, sf), (tph, tp), (prh, pr), (croph, crop), (pairh, pair))
    ):
        loads.append(pltpu.make_async_copy(src, dst, lsem.at[k]))
        loads[-1].start()

    loads[0].wait()
    tw = tf[...].astype(F32)
    tu = tw / jnp.sqrt(jnp.sum(tw * tw, axis=1, keepdims=True) + EPS)
    teach[pi, 0:4, :] = tu[:, 0:128].astype(BF16).astype(F32)
    teach[pi, 4:8, :] = tu[:, 128:256].astype(BF16).astype(F32)
    loads[1].wait()
    sw = sf[...].astype(F32)
    sn = jnp.sqrt(jnp.sum(sw * sw, axis=1, keepdims=True) + EPS)
    sd = sw / sn
    snorm[...] = jnp.broadcast_to(sn, (OWN, 128))
    sdir[...] = sd
    pack[...] = jnp.zeros_like(pack)
    hsend[...] = jnp.zeros_like(hsend)
    pack[0:OWN, :] = sd[:, 0:128]
    pack[24 : 24 + OWN, :] = sd[:, 128:256]
    stud[py, pz] = pack[...].astype(BF16)

    loads[2].wait()

    @pl.loop(0, C // 256)
    def _(j):
        cols = pl.ds(pl.multiple_of(j * 256, 256), 256)
        v = tp[:, cols].astype(F32)
        inv = 1.0 / jnp.sqrt(jnp.sum(v * v, axis=0, keepdims=True) + EPS)
        tpb[:, cols] = (v * inv).astype(BF16)

    pl.semaphore_wait(barrier, NPR - 1 + NDP - 1)
    send(X_TEACH, "proto", teach)
    send(X_STUDZ, "z", stud.at[py])

    loads[3].wait()

    @pl.loop(0, C // 256)
    def _(j):
        cols = pl.ds(pl.multiple_of(j * 256, 256), 256)
        v = pr[:, cols].astype(F32)
        n = jnp.sqrt(jnp.sum(v * v, axis=0, keepdims=True) + EPS)
        pnorm[:, cols] = n
        wb[:, cols] = (v * (1.0 / n)).astype(BF16)

    loads[4].wait()
    loads[5].wait()
    lanes = lax.broadcasted_iota(jnp.int32, (128, 128), 1).astype(F32)
    base = (dp * IMG_DEV).astype(F32)
    for i in range(R // 128):
        image = row_to_columns(crop[i : i + 1, :].astype(F32)) - base
        w0 = row_to_columns(pair[0:1, 128 * i : 128 * i + 128].astype(F32))
        w1 = row_to_columns(pair[1:2, 128 * i : 128 * i + 128].astype(F32))
        sel = jnp.where(lanes == 2.0 * image, w0, 0.0) + jnp.where(lanes == 2.0 * image + 1.0, w1, 0.0)
        selb[128 * i : 128 * i + 128, :] = sel.astype(BF16)
        scalec[128 * i : 128 * i + 128, :] = w0 + w1
    own_rows = lax.broadcasted_iota(jnp.int32, (32, R), 0) + pi * OWN
    ownsel[...] = (lax.broadcasted_iota(jnp.int32, (32, R), 1) == own_rows).astype(F32)

    arrived(X_TEACH, "proto", teach)
    for p in range(NPR):
        v = teach[p]
        x32[4 * p : 4 * p + 4, 0:128] = v[0:4]
        x32[4 * p : 4 * p + 4, 128:256] = v[4:8]
    tgrp[dp] = x32[0:T, :].astype(BF16)

    def assign(g):
        rows = tgrp[g]
        for j in range(C // CH):
            e = jnp.exp(dot(rows, tpb[:, CH * j : CH * j + CH]) * TEACHER_SCALE)
            ass[group_rows(g), CH * j : CH * j + CH] = e

    assign(dp)

    def column_part(g, acc, arow, table=ass):
        if arow is not None:
            wide = row_to_columns(arow)
        for i in range(T // 8):
            e = table[pl.ds(pl.multiple_of(g * T + 8 * i, 8), 8), :]
            if arow is not None:
                e = e * jnp.concatenate([wide[8 * i : 8 * i + 8]] * (C // 128), axis=1)
            acc = acc + e
        return acc

    def row_part(g):
        cb = jnp.broadcast_to(cvec[...], (8, C))
        parts = []
        for i in range(T // 8):
            parts.append(lane_tiles(ass[pl.ds(pl.multiple_of(g * T + 8 * i, 8), 8), :] * cb))
        return columns_to_row(jnp.concatenate(parts, axis=0))

    col1[dp] = jnp.sum(column_part(dp, jnp.zeros((8, C), F32), None), axis=0, keepdims=True)
    send(X_COL1, "dp", col1)
    send(X_TGRP, "dp", tgrp)
    arrived(X_STUDZ, "z", stud.at[py])
    send(X_STUDY, "y", stud)

    arrived(X_COL1, "dp", col1)
    cvec[...] = 1.0 / jnp.sum(col1[...], axis=0)
    row1[pi] = row_part(dp)
    send(X_ROW1, "proto", row1)

    arrived(X_STUDY, "y", stud)
    for p in range(NPR):
        v = stud[p % 4, p // 4].astype(F32)
        x32[OWN * p : OWN * p + OWN, 0:128] = v[0:OWN]
        x32[OWN * p : OWN * p + OWN, 128:256] = v[24 : 24 + OWN]
    xb[...] = x32[...].astype(BF16)
    for i in range(R // 128):
        xt[:, 128 * i : 128 * i + 128] = jnp.transpose(x32[128 * i : 128 * i + 128, :]).astype(BF16)

    @pl.loop(0, R // 128)
    def _(i):
        rows = pl.ds(pl.multiple_of(i * 128, 128), 128)
        part = jnp.zeros((128, 128), F32)
        for j in range(C // CH):
            e = jnp.exp(dot(xb[rows, :], wb[:, CH * j : CH * j + CH]) * STUDENT_SCALE)
            expo[rows, CH * j : CH * j + CH] = e
            expb[rows, CH * j : CH * j + CH] = e.astype(BF16)
            part = part + lane_tiles(e)
        tot[pi, pl.ds(i, 1), :] = columns_to_row(part)

    tot[pi, 5:8, :] = jnp.ones((3, 128), F32)

    arrived(X_ROW1, "proto", row1)
    avec[0:1, :] = 1.0 / jnp.sum(row1[...], axis=0)
    col2[dp] = jnp.sum(column_part(dp, jnp.zeros((8, C), F32), avec[0:1, :]), axis=0, keepdims=True)
    send(X_COL2, "dp", col2)
    send(X_TOT, "proto", tot)

    @pl.loop(0, R // 128)
    def _(i):
        rows = pl.ds(pl.multiple_of(i * 128, 128), 128)
        harr[rows, :] = dot_nt(expb[rows, :], wb[...])

    for p in range(NPR):
        for half in range(2):
            hsend[half, p % 4, p // 4, 0:OWN, :] = harr[OWN * p : OWN * p + OWN, 128 * half : 128 * half + 128]
    send(X_HY0, "y", hybuf.at[0], hsend.at[0])
    for half in range(2):
        hybuf[half, py] = hsend[half, py]

    def half_sums(half, x, y):
        arrived(x, "y", hybuf.at[half])
        for z in range(8):
            hzsend[half, z] = jnp.sum(hybuf[half, :, z], axis=0)
        send(y, "z", hzbuf.at[half], hzsend.at[half])
        hzbuf[half, pz] = hzsend[half, pz]

    arrived(X_TGRP, "dp", tgrp)

    @pl.loop(1, NDP)
    def _(i):
        assign(lax.rem(dp + i, NDP))

    def columns():
        acc = lax.fori_loop(
            0, NDP, lambda g, acc: column_part(g, acc, avec[pl.ds(g, 1), :]), jnp.zeros((8, C), F32)
        )
        cvec[...] = 1.0 / jnp.sum(acc, axis=0, keepdims=True)

    def rows_into(buf):
        @pl.loop(0, NDP)
        def _(g):
            buf[pi, pl.ds(g, 1), :] = row_part(g)

    arrived(X_COL2, "dp", col2)
    cvec[...] = 1.0 / jnp.sum(col2[...], axis=0)
    rows_into(row2)
    send(X_ROW2, "proto", row2)
    send(X_HY1, "y", hybuf.at[1], hsend.at[1])

    half_sums(0, X_HY0, X_HZ0)

    ut = dot(xt[...], selb[...])
    for g in range(NDP):
        utsend[g] = ut[32 * g : 32 * g + 32, :]
    send(X_UT, "dp", utbuf, utsend)
    utbuf[dp] = utsend[dp]

    arrived(X_TOT, "proto", tot)
    inv_tot = 1.0 / jnp.sum(tot[...], axis=0)
    for i in range(R // 128):
        rows = slice(128 * i, 128 * i + 128)
        scalec[rows, :] = scalec[rows, :] * row_to_columns(inv_tot[i : i + 1, :])

    @pl.loop(0, R // 16)
    def _(i):
        rows = pl.ds(pl.multiple_of(i * 16, 16), 16)
        s = scalec[rows, :]
        probb[rows, :] = (expo[rows, :] * jnp.concatenate([s] * (C // 128), axis=1)).astype(BF16)

    for j in range(C // CH):
        cols = slice(CH * j, CH * j + CH)
        pg = dot(xt[...], probb[:, cols])
        direction = pr[:, cols].astype(F32) / pnorm[:, cols]
        pg = (pg - direction * jnp.sum(direction * pg, axis=0, keepdims=True)).astype(BF16)
        for g in range(NDP):
            pgsend[g, :, cols] = pg[32 * g : 32 * g + 32, :]
    send(X_PG, "dp", pgbuf, pgsend)
    pgbuf[dp] = pgsend[dp]

    ur = jnp.transpose(ut)
    utb = ur.astype(BF16)
    utb = jnp.concatenate([utb, (ur - utb.astype(F32)).astype(BF16)], axis=0)
    for j in range(C // CH):
        cols = slice(CH * j, CH * j + CH)
        along = dot(utb, wb[:, cols])
        along = along[0:T] + along[T : 2 * T]
        mown[:, cols] = along * ass[group_rows(dp), cols]

    arrived(X_ROW2, "proto", row2)
    avec[...] = 1.0 / jnp.sum(row2[...], axis=0)
    columns()
    half_sums(1, X_HY1, X_HZ1)

    cb = jnp.broadcast_to(cvec[...], (16, C))
    for i in range(T // 16):
        rows = pl.ds(pl.multiple_of(dp * T + 16 * i, 16), 16)
        probb[16 * i : 16 * i + 16, :] = (ass[rows, :] * cb).astype(BF16)
    garr[...] = dot_nt(probb[0:T, :], wb[...])
    for p in range(16):
        gsend[p] = garr[8 * p : 8 * p + 8, 0:128]
        gsend[p + 16] = garr[8 * p : 8 * p + 8, 128:256]
    send(X_G, "proto", gbuf, gsend)
    gbuf[pi] = gsend[pi]
    rows_into(row3)
    send(X_ROW3, "proto", row3)


    arrived(X_HZ0, "z", hzbuf.at[0])
    arrived(X_HZ1, "z", hzbuf.at[1])
    hsum = jnp.sum(hzbuf[...], axis=1)
    own_scale = jnp.dot(ownsel[...], scalec[...], precision=lax.Precision.HIGHEST, preferred_element_type=F32)[0:OWN, 0:1]
    own_pick = dot(ownsel[...].astype(BF16), selb[...])[0:OWN, :]

    @pl.loop(0, NDP * T // 32)
    def _(i):
        rows = pl.ds(pl.multiple_of(i * 32, 32), 32)
        assb[rows, :] = ass[rows, :].astype(BF16)

    arrived(X_G, "proto", gbuf)
    gall[pi] = jnp.sum(gbuf[...], axis=0)
    send(X_GALL, "proto", gall)

    arrived(X_ROW3, "proto", row3)
    avec[...] = 1.0 / jnp.sum(row3[...], axis=0)
    along = jnp.sum(column_part(0, jnp.zeros((8, C), F32), avec[pl.ds(dp, 1), :], mown), axis=0, keepdims=True)
    dotbuf[dp] = along * cvec[...]
    send(X_DOT, "dp", dotbuf)
    arrived(X_UT, "dp", utbuf)
    lhs = jnp.concatenate([utbuf[g] * avec[g : g + 1, :] for g in range(NDP)], axis=1)
    high = lhs.astype(BF16)
    lhs = jnp.concatenate([high, (lhs - high.astype(F32)).astype(BF16)], axis=0)
    arrived(X_PG, "dp", pgbuf)
    own32 = pl.ds(pl.multiple_of(dp * 32, 32), 32)
    for j in range(C // CH):
        cols = slice(CH * j, CH * j + CH)
        both = dot(lhs, assb[:, cols])
        target = (both[0:32] + both[32:64]) * cvec[:, cols]
        own = GRAD_SCALE * (jnp.sum(pgbuf[:, :, cols].astype(F32), axis=0) - target)
        pown[:, cols] = own

    arrived(X_DOT, "dp", dotbuf)
    for j in range(C // CH):
        cols = slice(CH * j, CH * j + CH)
        column_dot = -GRAD_SCALE * jnp.sum(dotbuf[:, :, cols], axis=0)
        inv = 1.0 / pnorm[:, cols]
        pown[:, cols] = (pown[:, cols] - pr[own32, cols].astype(F32) * (inv * column_dot)) * inv
    store = pltpu.make_async_copy(pown, pgrad, lsem.at[6])
    store.start()

    arrived(X_GALL, "proto", gall)
    gfull = jnp.concatenate([gall[0:16].reshape(T, 128), gall[16:32].reshape(T, 128)], axis=1)
    picked = jnp.dot(
        own_pick * avec[pl.ds(dp, 1), :], gfull, precision=lax.Precision.HIGHEST, preferred_element_type=F32
    )
    h = jnp.concatenate([hsum[0, 0:OWN], hsum[1, 0:OWN]], axis=1)
    unit_grad = GRAD_SCALE * (own_scale * h - picked)
    sd = sdir[...]
    sgrad[...] = (unit_grad - sd * jnp.sum(sd * unit_grad, axis=1, keepdims=True)) / snorm[:, 0:1]

    store.wait()
    for x, axis, buf in (
        (X_TEACH, "proto", teach), (X_STUDZ, "z", stud.at[py]), (X_STUDY, "y", stud), (X_COL1, "dp", col1),
        (X_TGRP, "dp", tgrp), (X_ROW1, "proto", row1), (X_COL2, "dp", col2), (X_TOT, "proto", tot),
        (X_ROW2, "proto", row2), (X_HY0, "y", hybuf.at[0]), (X_HY1, "y", hybuf.at[1]),
        (X_HZ0, "z", hzbuf.at[0]), (X_HZ1, "z", hzbuf.at[1]), (X_UT, "dp", utbuf), (X_ROW3, "proto", row3),
        (X_G, "proto", gbuf), (X_PG, "dp", pgbuf), (X_GALL, "proto", gall), (X_DOT, "dp", dotbuf),
    ):
        sent(x, axis, buf)


def last_step(student, proto, sgrad, pgrad):
    sgrad[...] = student[...]
    pgrad[...] = proto[...]


def per_device(student_feats, teacher_feats, prototypes, teacher_prototypes, crop_image, pairing):
    vmem = pl.BlockSpec(memory_space=pltpu.VMEM)
    anywhere = pl.BlockSpec(memory_space=pl.ANY)
    outs = (jax.ShapeDtypeStruct((OWN, K), F32), jax.ShapeDtypeStruct((K // NDP, C), F32))
    student, proto = pl.pallas_call(
        kernel,
        out_shape=outs,
        in_specs=[anywhere] * 6,
        out_specs=(vmem, anywhere),
        scratch_shapes=[
            pltpu.VMEM((NPR, 8, 128), F32),
            pltpu.VMEM((4, 8, PAD, 128), BF16),
            pltpu.VMEM((NDP, 1, C), F32),
            pltpu.VMEM((NDP, T, K), BF16),
            pltpu.VMEM((NPR, 1, 128), F32),
            pltpu.VMEM((NDP, 1, C), F32),
            pltpu.VMEM((NPR, 8, 128), F32),
            pltpu.VMEM((NPR, 8, 128), F32),
            pltpu.VMEM((2, 4, 8, HPAD, 128), F32),
            pltpu.VMEM((2, 8, HPAD, 128), F32),
            pltpu.VMEM((NDP, 32, 128), F32),
            pltpu.VMEM((NPR, 8, 128), F32),
            pltpu.VMEM((NPR, 8, 128), F32),
            pltpu.VMEM((NDP, 32, C), BF16),
            pltpu.VMEM((NPR, 8, 128), F32),
            pltpu.VMEM((NDP, 1, C), F32),
            pltpu.VMEM((2, 4, 8, HPAD, 128), F32),
            pltpu.VMEM((2, 8, HPAD, 128), F32),
            pltpu.VMEM((NDP, 32, 128), F32),
            pltpu.VMEM((NPR, 8, 128), F32),
            pltpu.VMEM((NDP, 32, C), BF16),
            pltpu.VMEM((PAD, 128), F32),
            pltpu.VMEM((R, K), F32),
            pltpu.VMEM((R, K), BF16),
            pltpu.VMEM((K, R), BF16),
            pltpu.VMEM((K, C), BF16),
            pltpu.VMEM((K, C), BF16),
            pltpu.VMEM((1, C), F32),
            pltpu.VMEM((K // NDP, C), F32),
            pltpu.VMEM((R, C), F32),
            pltpu.VMEM((R, C), BF16),
            pltpu.VMEM((R, C), BF16),
            pltpu.VMEM((R, 128), BF16),
            pltpu.VMEM((R, 128), F32),
            pltpu.VMEM((R, K), F32),
            pltpu.VMEM((T, K), F32),
            pltpu.VMEM((NDP * T, C), F32),
            pltpu.VMEM((NDP * T, C), BF16),
            pltpu.VMEM((T, C), F32),
            pltpu.VMEM((1, C), F32),
            pltpu.VMEM((8, 128), F32),
            pltpu.VMEM((OWN, K), F32),
            pltpu.VMEM((OWN, 128), F32),
            pltpu.VMEM((32, R), F32),
            pltpu.VMEM((OWN, K), BF16),
            pltpu.VMEM((4, K), BF16),
            pltpu.VMEM((K, C), BF16),
            pltpu.VMEM((K, C), BF16),
            pltpu.VMEM((R // 128, 128), jnp.int32),
            pltpu.VMEM((2, R), jnp.int32),
            pltpu.SemaphoreType.DMA((N_X,)),
            pltpu.SemaphoreType.DMA((N_X,)),
            pltpu.SemaphoreType.DMA((7,)),
        ],
        compiler_params=pltpu.CompilerParams(
            collective_id=0, has_side_effects=True, vmem_limit_bytes=56 * 2**20
        ),
    )(student_feats, teacher_feats, prototypes, teacher_prototypes, crop_image.reshape(R // 128, 128), pairing.T)
    return pl.pallas_call(
        last_step,
        out_shape=outs,
        in_specs=[vmem] * 2,
        out_specs=(vmem, vmem),
        compiler_params=pltpu.CompilerParams(vmem_limit_bytes=56 * 2**20),
    )(student, proto)


def solution(mesh):
    in_specs = (
        P(("dp", "proto"), None),
        P(("dp", "proto"), None),
        P(None, "proto"),
        P(None, "proto"),
        P("dp"),
        P("dp", None),
    )
    out_specs = (P(("dp", "proto"), None), P("dp", "proto"))
    return jax.shard_map(
        per_device, mesh=mesh, in_specs=in_specs, out_specs=out_specs, check_vma=False
    )
```

```python
import jax
import jax.numpy as jnp
from jax import lax
from jax.experimental import pallas as pl
from jax.experimental.pallas import tpu as pltpu
from jax.sharding import PartitionSpec as P

MESH = pl.DeviceIdType.MESH
F32 = jnp.float32
BF16 = jnp.bfloat16

IMG_DEV = 64
EPS = 1e-06
TEACHER_SCALE = 1.0 / 0.07
STUDENT_SCALE = 1.0 / 0.1
GRAD_SCALE = 4096.0 / 0.1

NDP = 8
NPR = 32
K = 256
C = 2048
R = 640
T = 128
OWN = 20
PAD = 48
HPAD = 24
CH = 512

(
    X_TEACH, X_STUDZ, X_STUDY, X_COL1, X_TGRP, X_ROW1, X_COL2, X_TOT, X_ROW2, X_HY0, X_HY1, X_HZ0, X_HZ1, X_UT, X_ROW3, X_G, X_PG, X_GALL, X_DOT
) = range(19)
N_X = 19
SIZES = {"dp": 8, "proto": 32, "z": 8, "y": 4}


def row_to_columns(row):
    return jnp.transpose(jnp.broadcast_to(row, (128, 128)))


def columns_to_row(part):
    return jnp.sum(jnp.transpose(part), axis=0, keepdims=True)


def lane_tiles(value):
    total = value[:, 0:128]
    for j in range(1, value.shape[1] // 128):
        total = total + value[:, 128 * j : 128 * j + 128]
    return total


def dot(a, b):
    return jnp.dot(a, b, preferred_element_type=F32)


def dot_nt(a, b):
    return lax.dot_general(a, b, (((1,), (1,)), ((), ())), preferred_element_type=F32)


def kernel(
    sfh, tfh, prh, tph, croph, pairh,
    sgrad, pgrad,
    teach, stud, col1, tgrp, row1, col2, tot, row2, hybuf, hzbuf, utbuf, row3, gbuf, pgbuf, gall, dotbuf,
    hsend, hzsend, utsend, gsend, pgsend,
    pack, x32, xb, xt, wb, tpb, pnorm, pown, expo, expb, probb, selb, scalec, harr, garr, ass, assb, mown, cvec, avec,
    sdir, snorm, ownsel, sf, tf, pr, tp, crop, pair,
    ssem, rsem, lsem,
):
    dp = lax.axis_index("dp")
    pi = lax.axis_index("proto")

    pz, py = pi // 4, lax.rem(pi, 4)

    def far_first(i, half):
        return half + ((i + 1) // 2) * (1 - 2 * lax.rem(i, 2))

    def peer(axis, i):
        if axis == "dp":
            return lax.rem(dp + i + 1, NDP)
        if axis == "z":
            return lax.rem(pz + far_first(i, 4), 8)
        if axis == "y":
            return lax.rem(py + far_first(i, 2), 4)
        return lax.rem(pz + far_first(i // 4, 4), 8) * 4 + lax.rem(py + far_first(lax.rem(i, 4), 2), 4)

    def address(axis, p):
        if axis == "dp":
            return (p, pi)
        if axis == "z":
            return (dp, p * 4 + py)
        if axis == "y":
            return (dp, pz * 4 + p)
        return (dp, p)

    def mine(axis):
        return {"dp": dp, "proto": pi, "z": pz, "y": py}[axis]

    def count(axis):
        return SIZES[axis]

    def send(x, axis, dst, src=None):
        me = mine(axis)

        @pl.loop(0, count(axis) - 1)
        def _(i):
            p = peer(axis, i)
            pltpu.make_async_remote_copy(
                src_ref=dst.at[me] if src is None else src.at[p],
                dst_ref=dst.at[me],
                send_sem=ssem.at[x],
                recv_sem=rsem.at[x],
                device_id=address(axis, p),
                device_id_type=MESH,
            ).start()

    def arrived(x, axis, dst):
        blocks = dst.at[pl.ds(0, count(axis) - 1)]
        pltpu.make_async_copy(blocks, blocks, rsem.at[x]).wait()

    def sent(x, axis, dst):
        blocks = dst.at[pl.ds(0, count(axis) - 1)]
        pltpu.make_async_copy(blocks, blocks, ssem.at[x]).wait()

    def group_rows(g):
        return pl.ds(pl.multiple_of(g * T, T), T)

    barrier = pltpu.get_barrier_semaphore()
    for axis in ("proto", "dp"):
        @pl.loop(0, count(axis) - 1)
        def _(i, axis=axis):
            p = peer(axis, i)
            pl.semaphore_signal(barrier, inc=1, device_id=address(axis, p), device_id_type=MESH)

    loads = []
    for k, (src, dst) in enumerate(
        ((tfh, tf), (sfh, sf), (tph, tp), (prh, pr), (croph, crop), (pairh, pair))
    ):
        loads.append(pltpu.make_async_copy(src, dst, lsem.at[k]))
        loads[-1].start()

    loads[0].wait()
    tw = tf[...].astype(F32)
    tu = tw / jnp.sqrt(jnp.sum(tw * tw, axis=1, keepdims=True) + EPS)
    teach[pi, 0:4, :] = tu[:, 0:128].astype(BF16).astype(F32)
    teach[pi, 4:8, :] = tu[:, 128:256].astype(BF16).astype(F32)
    loads[1].wait()
    sw = sf[...].astype(F32)
    sn = jnp.sqrt(jnp.sum(sw * sw, axis=1, keepdims=True) + EPS)
    sd = sw / sn
    snorm[...] = jnp.broadcast_to(sn, (OWN, 128))
    sdir[...] = sd
    pack[...] = jnp.zeros_like(pack)
    hsend[...] = jnp.zeros_like(hsend)
    pack[0:OWN, :] = sd[:, 0:128]
    pack[24 : 24 + OWN, :] = sd[:, 128:256]
    stud[py, pz] = pack[...].astype(BF16)

    loads[2].wait()

    @pl.loop(0, C // 256)
    def _(j):
        cols = pl.ds(pl.multiple_of(j * 256, 256), 256)
        v = tp[:, cols].astype(F32)
        inv = 1.0 / jnp.sqrt(jnp.sum(v * v, axis=0, keepdims=True) + EPS)
        tpb[:, cols] = (v * inv).astype(BF16)

    pl.semaphore_wait(barrier, NPR - 1 + NDP - 1)
    send(X_TEACH, "proto", teach)
    send(X_STUDZ, "z", stud.at[py])

    loads[3].wait()

    @pl.loop(0, C // 256)
    def _(j):
        cols = pl.ds(pl.multiple_of(j * 256, 256), 256)
        v = pr[:, cols].astype(F32)
        n = jnp.sqrt(jnp.sum(v * v, axis=0, keepdims=True) + EPS)
        pnorm[:, cols] = n
        wb[:, cols] = (v * (1.0 / n)).astype(BF16)

    loads[4].wait()
    loads[5].wait()
    lanes = lax.broadcasted_iota(jnp.int32, (128, 128), 1).astype(F32)
    base = (dp * IMG_DEV).astype(F32)
    for i in range(R // 128):
        image = row_to_columns(crop[i : i + 1, :].astype(F32)) - base
        w0 = row_to_columns(pair[0:1, 128 * i : 128 * i + 128].astype(F32))
        w1 = row_to_columns(pair[1:2, 128 * i : 128 * i + 128].astype(F32))
        sel = jnp.where(lanes == 2.0 * image, w0, 0.0) + jnp.where(lanes == 2.0 * image + 1.0, w1, 0.0)
        selb[128 * i : 128 * i + 128, :] = sel.astype(BF16)
        scalec[128 * i : 128 * i + 128, :] = w0 + w1
    own_rows = lax.broadcasted_iota(jnp.int32, (32, R), 0) + pi * OWN
    ownsel[...] = (lax.broadcasted_iota(jnp.int32, (32, R), 1) == own_rows).astype(F32)

    arrived(X_TEACH, "proto", teach)
    for p in range(NPR):
        v = teach[p]
        x32[4 * p : 4 * p + 4, 0:128] = v[0:4]
        x32[4 * p : 4 * p + 4, 128:256] = v[4:8]
    tgrp[dp] = x32[0:T, :].astype(BF16)

    def assign(g):
        rows = tgrp[g]
        for j in range(C // CH):
            e = jnp.exp(dot(rows, tpb[:, CH * j : CH * j + CH]) * TEACHER_SCALE)
            ass[group_rows(g), CH * j : CH * j + CH] = e

    assign(dp)

    def column_part(g, acc, arow, table=ass):
        if arow is not None:
            wide = row_to_columns(arow)
        for i in range(T // 8):
            e = table[pl.ds(pl.multiple_of(g * T + 8 * i, 8), 8), :]
            if arow is not None:
                e = e * jnp.concatenate([wide[8 * i : 8 * i + 8]] * (C // 128), axis=1)
            acc = acc + e
        return acc

    def row_part(g):
        cb = jnp.broadcast_to(cvec[...], (8, C))
        parts = []
        for i in range(T // 8):
            parts.append(lane_tiles(ass[pl.ds(pl.multiple_of(g * T + 8 * i, 8), 8), :] * cb))
        return columns_to_row(jnp.concatenate(parts, axis=0))

    col1[dp] = jnp.sum(column_part(dp, jnp.zeros((8, C), F32), None), axis=0, keepdims=True)
    send(X_COL1, "dp", col1)
    send(X_TGRP, "dp", tgrp)
    arrived(X_STUDZ, "z", stud.at[py])
    send(X_STUDY, "y", stud)

    arrived(X_COL1, "dp", col1)
    cvec[...] = 1.0 / jnp.sum(col1[...], axis=0)
    row1[pi] = row_part(dp)
    send(X_ROW1, "proto", row1)

    arrived(X_STUDY, "y", stud)
    for p in range(NPR):
        v = stud[p % 4, p // 4].astype(F32)
        x32[OWN * p : OWN * p + OWN, 0:128] = v[0:OWN]
        x32[OWN * p : OWN * p + OWN, 128:256] = v[24 : 24 + OWN]
    xb[...] = x32[...].astype(BF16)
    for i in range(R // 128):
        xt[:, 128 * i : 128 * i + 128] = jnp.transpose(x32[128 * i : 128 * i + 128, :]).astype(BF16)

    @pl.loop(0, R // 128)
    def _(i):
        rows = pl.ds(pl.multiple_of(i * 128, 128), 128)
        part = jnp.zeros((128, 128), F32)
        for j in range(C // CH):
            e = jnp.exp(dot(xb[rows, :], wb[:, CH * j : CH * j + CH]) * STUDENT_SCALE)
            expo[rows, CH * j : CH * j + CH] = e
            expb[rows, CH * j : CH * j + CH] = e.astype(BF16)
            part = part + lane_tiles(e)
        tot[pi, pl.ds(i, 1), :] = columns_to_row(part)

    tot[pi, 5:8, :] = jnp.ones((3, 128), F32)

    @pl.loop(0, R // 128)
    def _(i):
        rows = pl.ds(pl.multiple_of(i * 128, 128), 128)
        harr[rows, :] = dot_nt(expb[rows, :], wb[...])

    for p in range(NPR):
        for half in range(2):
            hsend[half, p % 4, p // 4, 0:OWN, :] = harr[OWN * p : OWN * p + OWN, 128 * half : 128 * half + 128]
    for half in range(2):
        hybuf[half, py] = hsend[half, py]

    arrived(X_ROW1, "proto", row1)
    avec[0:1, :] = 1.0 / jnp.sum(row1[...], axis=0)
    col2[dp] = jnp.sum(column_part(dp, jnp.zeros((8, C), F32), avec[0:1, :]), axis=0, keepdims=True)
    send(X_COL2, "dp", col2)
    send(X_HY0, "y", hybuf.at[0], hsend.at[0])
    send(X_TOT, "proto", tot)

    def half_sums(half, x, y):
        arrived(x, "y", hybuf.at[half])
        for z in range(8):
            hzsend[half, z] = jnp.sum(hybuf[half, :, z], axis=0)
        send(y, "z", hzbuf.at[half], hzsend.at[half])
        hzbuf[half, pz] = hzsend[half, pz]

    arrived(X_TGRP, "dp", tgrp)

    @pl.loop(1, NDP)
    def _(i):
        assign(lax.rem(dp + i, NDP))

    def columns():
        acc = lax.fori_loop(
            0, NDP, lambda g, acc: column_part(g, acc, avec[pl.ds(g, 1), :]), jnp.zeros((8, C), F32)
        )
        cvec[...] = 1.0 / jnp.sum(acc, axis=0, keepdims=True)

    def rows_into(buf):
        @pl.loop(0, NDP)
        def _(g):
            buf[pi, pl.ds(g, 1), :] = row_part(g)

    arrived(X_COL2, "dp", col2)
    cvec[...] = 1.0 / jnp.sum(col2[...], axis=0)
    rows_into(row2)
    send(X_ROW2, "proto", row2)
    send(X_HY1, "y", hybuf.at[1], hsend.at[1])

    half_sums(0, X_HY0, X_HZ0)

    ut = dot(xt[...], selb[...])
    for g in range(NDP):
        utsend[g] = ut[32 * g : 32 * g + 32, :]
    send(X_UT, "dp", utbuf, utsend)
    utbuf[dp] = utsend[dp]

    arrived(X_TOT, "proto", tot)
    inv_tot = 1.0 / jnp.sum(tot[...], axis=0)
    for i in range(R // 128):
        rows = slice(128 * i, 128 * i + 128)
        scalec[rows, :] = scalec[rows, :] * row_to_columns(inv_tot[i : i + 1, :])

    @pl.loop(0, R // 16)
    def _(i):
        rows = pl.ds(pl.multiple_of(i * 16, 16), 16)
        s = scalec[rows, :]
        probb[rows, :] = (expo[rows, :] * jnp.concatenate([s] * (C // 128), axis=1)).astype(BF16)

    for j in range(C // CH):
        cols = slice(CH * j, CH * j + CH)
        pg = dot(xt[...], probb[:, cols])
        direction = pr[:, cols].astype(F32) / pnorm[:, cols]
        pg = (pg - direction * jnp.sum(direction * pg, axis=0, keepdims=True)).astype(BF16)
        for g in range(NDP):
            pgsend[g, :, cols] = pg[32 * g : 32 * g + 32, :]
    send(X_PG, "dp", pgbuf, pgsend)
    pgbuf[dp] = pgsend[dp]

    ur = jnp.transpose(ut)
    utb = ur.astype(BF16)
    utb = jnp.concatenate([utb, (ur - utb.astype(F32)).astype(BF16)], axis=0)
    for j in range(C // CH):
        cols = slice(CH * j, CH * j + CH)
        along = dot(utb, wb[:, cols])
        along = along[0:T] + along[T : 2 * T]
        mown[:, cols] = along * ass[group_rows(dp), cols].astype(BF16).astype(F32)

    arrived(X_ROW2, "proto", row2)
    avec[...] = 1.0 / jnp.sum(row2[...], axis=0)
    columns()

    cb = jnp.broadcast_to(cvec[...], (16, C))
    for i in range(T // 16):
        rows = pl.ds(pl.multiple_of(dp * T + 16 * i, 16), 16)
        probb[16 * i : 16 * i + 16, :] = (ass[rows, :] * cb).astype(BF16)
    garr[...] = dot_nt(probb[0:T, :], wb[...])
    for p in range(16):
        gsend[p] = garr[8 * p : 8 * p + 8, 0:128]
        gsend[p + 16] = garr[8 * p : 8 * p + 8, 128:256]
    send(X_G, "proto", gbuf, gsend)
    half_sums(1, X_HY1, X_HZ1)
    gbuf[pi] = gsend[pi]
    rows_into(row3)
    send(X_ROW3, "proto", row3)


    arrived(X_HZ0, "z", hzbuf.at[0])
    arrived(X_HZ1, "z", hzbuf.at[1])
    hsum = jnp.sum(hzbuf[...], axis=1)
    own_scale = jnp.dot(ownsel[...], scalec[...], precision=lax.Precision.HIGHEST, preferred_element_type=F32)[0:OWN, 0:1]
    own_pick = dot(ownsel[...].astype(BF16), selb[...])[0:OWN, :]

    @pl.loop(0, NDP * T // 32)
    def _(i):
        rows = pl.ds(pl.multiple_of(i * 32, 32), 32)
        assb[rows, :] = ass[rows, :].astype(BF16)

    arrived(X_G, "proto", gbuf)
    gall[pi] = jnp.sum(gbuf[...], axis=0)
    send(X_GALL, "proto", gall)

    arrived(X_ROW3, "proto", row3)
    avec[...] = 1.0 / jnp.sum(row3[...], axis=0)
    along = jnp.sum(column_part(0, jnp.zeros((8, C), F32), avec[pl.ds(dp, 1), :], mown), axis=0, keepdims=True)
    dotbuf[dp] = along * cvec[...]
    send(X_DOT, "dp", dotbuf)
    arrived(X_UT, "dp", utbuf)
    lhs = jnp.concatenate([utbuf[g] * avec[g : g + 1, :] for g in range(NDP)], axis=1)
    high = lhs.astype(BF16)
    lhs = jnp.concatenate([high, (lhs - high.astype(F32)).astype(BF16)], axis=0)
    arrived(X_PG, "dp", pgbuf)
    own32 = pl.ds(pl.multiple_of(dp * 32, 32), 32)
    for j in range(C // CH):
        cols = slice(CH * j, CH * j + CH)
        both = dot(lhs, assb[:, cols])
        target = (both[0:32] + both[32:64]) * cvec[:, cols]
        own = GRAD_SCALE * (jnp.sum(pgbuf[:, :, cols].astype(F32), axis=0) - target)
        pown[:, cols] = own

    arrived(X_DOT, "dp", dotbuf)
    for j in range(C // CH):
        cols = slice(CH * j, CH * j + CH)
        column_dot = -GRAD_SCALE * jnp.sum(dotbuf[:, :, cols], axis=0)
        inv = 1.0 / pnorm[:, cols]
        pown[:, cols] = (pown[:, cols] - pr[own32, cols].astype(F32) * (inv * column_dot)) * inv
    store = pltpu.make_async_copy(pown, pgrad, lsem.at[6])
    store.start()

    arrived(X_GALL, "proto", gall)
    gfull = jnp.concatenate([gall[0:16].reshape(T, 128), gall[16:32].reshape(T, 128)], axis=1)
    picked = jnp.dot(
        own_pick * avec[pl.ds(dp, 1), :], gfull, precision=lax.Precision.HIGHEST, preferred_element_type=F32
    )
    h = jnp.concatenate([hsum[0, 0:OWN], hsum[1, 0:OWN]], axis=1)
    unit_grad = GRAD_SCALE * (own_scale * h - picked)
    sd = sdir[...]
    sgrad[...] = (unit_grad - sd * jnp.sum(sd * unit_grad, axis=1, keepdims=True)) / snorm[:, 0:1]

    store.wait()
    for x, axis, buf in (
        (X_TEACH, "proto", teach), (X_STUDZ, "z", stud.at[py]), (X_STUDY, "y", stud), (X_COL1, "dp", col1),
        (X_TGRP, "dp", tgrp), (X_ROW1, "proto", row1), (X_COL2, "dp", col2), (X_TOT, "proto", tot),
        (X_ROW2, "proto", row2), (X_HY0, "y", hybuf.at[0]), (X_HY1, "y", hybuf.at[1]),
        (X_HZ0, "z", hzbuf.at[0]), (X_HZ1, "z", hzbuf.at[1]), (X_UT, "dp", utbuf), (X_ROW3, "proto", row3),
        (X_G, "proto", gbuf), (X_PG, "dp", pgbuf), (X_GALL, "proto", gall), (X_DOT, "dp", dotbuf),
    ):
        sent(x, axis, buf)


def last_step(student, proto, sgrad, pgrad):
    sgrad[...] = student[...]
    pgrad[...] = proto[...]


def per_device(student_feats, teacher_feats, prototypes, teacher_prototypes, crop_image, pairing):
    vmem = pl.BlockSpec(memory_space=pltpu.VMEM)
    anywhere = pl.BlockSpec(memory_space=pl.ANY)
    outs = (jax.ShapeDtypeStruct((OWN, K), F32), jax.ShapeDtypeStruct((K // NDP, C), F32))
    student, proto = pl.pallas_call(
        kernel,
        out_shape=outs,
        in_specs=[anywhere] * 6,
        out_specs=(vmem, anywhere),
        scratch_shapes=[
            pltpu.VMEM((NPR, 8, 128), F32),
            pltpu.VMEM((4, 8, PAD, 128), BF16),
            pltpu.VMEM((NDP, 1, C), F32),
            pltpu.VMEM((NDP, T, K), BF16),
            pltpu.VMEM((NPR, 1, 128), F32),
            pltpu.VMEM((NDP, 1, C), F32),
            pltpu.VMEM((NPR, 8, 128), F32),
            pltpu.VMEM((NPR, 8, 128), F32),
            pltpu.VMEM((2, 4, 8, HPAD, 128), F32),
            pltpu.VMEM((2, 8, HPAD, 128), F32),
            pltpu.VMEM((NDP, 32, 128), F32),
            pltpu.VMEM((NPR, 8, 128), F32),
            pltpu.VMEM((NPR, 8, 128), F32),
            pltpu.VMEM((NDP, 32, C), BF16),
            pltpu.VMEM((NPR, 8, 128), F32),
            pltpu.VMEM((NDP, 1, C), F32),
            pltpu.VMEM((2, 4, 8, HPAD, 128), F32),
            pltpu.VMEM((2, 8, HPAD, 128), F32),
            pltpu.VMEM((NDP, 32, 128), F32),
            pltpu.VMEM((NPR, 8, 128), F32),
            pltpu.VMEM((NDP, 32, C), BF16),
            pltpu.VMEM((PAD, 128), F32),
            pltpu.VMEM((R, K), F32),
            pltpu.VMEM((R, K), BF16),
            pltpu.VMEM((K, R), BF16),
            pltpu.VMEM((K, C), BF16),
            pltpu.VMEM((K, C), BF16),
            pltpu.VMEM((1, C), F32),
            pltpu.VMEM((K // NDP, C), F32),
            pltpu.VMEM((R, C), F32),
            pltpu.VMEM((R, C), BF16),
            pltpu.VMEM((R, C), BF16),
            pltpu.VMEM((R, 128), BF16),
            pltpu.VMEM((R, 128), F32),
            pltpu.VMEM((R, K), F32),
            pltpu.VMEM((T, K), F32),
            pltpu.VMEM((NDP * T, C), F32),
            pltpu.VMEM((NDP * T, C), BF16),
            pltpu.VMEM((T, C), F32),
            pltpu.VMEM((1, C), F32),
            pltpu.VMEM((8, 128), F32),
            pltpu.VMEM((OWN, K), F32),
            pltpu.VMEM((OWN, 128), F32),
            pltpu.VMEM((32, R), F32),
            pltpu.VMEM((OWN, K), BF16),
            pltpu.VMEM((4, K), BF16),
            pltpu.VMEM((K, C), BF16),
            pltpu.VMEM((K, C), BF16),
            pltpu.VMEM((R // 128, 128), jnp.int32),
            pltpu.VMEM((2, R), jnp.int32),
            pltpu.SemaphoreType.DMA((N_X,)),
            pltpu.SemaphoreType.DMA((N_X,)),
            pltpu.SemaphoreType.DMA((7,)),
        ],
        compiler_params=pltpu.CompilerParams(
            collective_id=0, has_side_effects=True, vmem_limit_bytes=56 * 2**20
        ),
    )(student_feats, teacher_feats, prototypes, teacher_prototypes, crop_image.reshape(R // 128, 128), pairing.T)
    return pl.pallas_call(
        last_step,
        out_shape=outs,
        in_specs=[vmem] * 2,
        out_specs=(vmem, vmem),
        compiler_params=pltpu.CompilerParams(vmem_limit_bytes=56 * 2**20),
    )(student, proto)


def solution(mesh):
    in_specs = (
        P(("dp", "proto"), None),
        P(("dp", "proto"), None),
        P(None, "proto"),
        P(None, "proto"),
        P("dp"),
        P("dp", None),
    )
    out_specs = (P(("dp", "proto"), None), P("dp", "proto"))
    return jax.shard_map(
        per_device, mesh=mesh, in_specs=in_specs, out_specs=out_specs, check_vma=False
    )
```

```python
import jax
import jax.numpy as jnp
from jax import lax
from jax.experimental import pallas as pl
from jax.experimental.pallas import tpu as pltpu
from jax.sharding import PartitionSpec as P

MESH = pl.DeviceIdType.MESH
F32 = jnp.float32
BF16 = jnp.bfloat16

IMG_DEV = 64
EPS = 1e-06
TEACHER_SCALE = 1.0 / 0.07
STUDENT_SCALE = 1.0 / 0.1
GRAD_SCALE = 4096.0 / 0.1

NDP = 8
NPR = 32
K = 256
C = 2048
R = 640
T = 128
OWN = 20
PAD = 48
HPAD = 24
CH = 512

(
    X_TEACH, X_STUDZ, X_STUDY, X_COL1, X_TGRP, X_ROW1, X_COL2, X_TOT, X_ROW2, X_HY0, X_HY1, X_HZ0, X_HZ1, X_UT, X_ROW3, X_G, X_PG, X_GALL, X_DOT
) = range(19)
N_X = 19
SIZES = {"dp": 8, "proto": 32, "z": 8, "y": 4}


def row_to_columns(row):
    return jnp.transpose(jnp.broadcast_to(row, (128, 128)))


def columns_to_row(part):
    return jnp.sum(jnp.transpose(part), axis=0, keepdims=True)


def lane_tiles(value):
    total = value[:, 0:128]
    for j in range(1, value.shape[1] // 128):
        total = total + value[:, 128 * j : 128 * j + 128]
    return total


def dot(a, b):
    return jnp.dot(a, b, preferred_element_type=F32)


def dot_nt(a, b):
    return lax.dot_general(a, b, (((1,), (1,)), ((), ())), preferred_element_type=F32)


def kernel(
    sfh, tfh, prh, tph, croph, pairh,
    sgrad, pgrad,
    teach, stud, col1, tgrp, row1, col2, tot, row2, hybuf, hzbuf, utbuf, row3, gbuf, pgbuf, gall, dotbuf,
    hsend, hzsend, utsend, gsend, pgsend,
    pack, x32, xb, xt, wb, tpb, pnorm, pown, expo, expb, probb, selb, scalec, harr, garr, ass, assb, mown, cvec, avec,
    sdir, snorm, ownsel, sf, tf, pr, tp, crop, pair,
    ssem, rsem, lsem,
):
    dp = lax.axis_index("dp")
    pi = lax.axis_index("proto")

    pz, py = pi // 4, lax.rem(pi, 4)

    def far_first(i, half):
        return half + ((i + 1) // 2) * (1 - 2 * lax.rem(i, 2))

    def peer(axis, i):
        if axis == "dp":
            return lax.rem(dp + i + 1, NDP)
        if axis == "z":
            return lax.rem(pz + far_first(i, 4), 8)
        if axis == "y":
            return lax.rem(py + far_first(i, 2), 4)
        return lax.rem(pz + far_first(i // 4, 4), 8) * 4 + lax.rem(py + far_first(lax.rem(i, 4), 2), 4)

    def address(axis, p):
        if axis == "dp":
            return (p, pi)
        if axis == "z":
            return (dp, p * 4 + py)
        if axis == "y":
            return (dp, pz * 4 + p)
        return (dp, p)

    def mine(axis):
        return {"dp": dp, "proto": pi, "z": pz, "y": py}[axis]

    def count(axis):
        return SIZES[axis]

    def send(x, axis, dst, src=None):
        me = mine(axis)

        @pl.loop(0, count(axis) - 1)
        def _(i):
            p = peer(axis, i)
            pltpu.make_async_remote_copy(
                src_ref=dst.at[me] if src is None else src.at[p],
                dst_ref=dst.at[me],
                send_sem=ssem.at[x],
                recv_sem=rsem.at[x],
                device_id=address(axis, p),
                device_id_type=MESH,
            ).start()

    def arrived(x, axis, dst):
        blocks = dst.at[pl.ds(0, count(axis) - 1)]
        pltpu.make_async_copy(blocks, blocks, rsem.at[x]).wait()

    def sent(x, axis, dst):
        blocks = dst.at[pl.ds(0, count(axis) - 1)]
        pltpu.make_async_copy(blocks, blocks, ssem.at[x]).wait()

    def group_rows(g):
        return pl.ds(pl.multiple_of(g * T, T), T)

    barrier = pltpu.get_barrier_semaphore()
    for axis in ("proto", "dp"):
        @pl.loop(0, count(axis) - 1)
        def _(i, axis=axis):
            p = peer(axis, i)
            pl.semaphore_signal(barrier, inc=1, device_id=address(axis, p), device_id_type=MESH)

    loads = []
    for k, (src, dst) in enumerate(
        ((tfh, tf), (sfh, sf), (tph, tp), (prh, pr), (croph, crop), (pairh, pair))
    ):
        loads.append(pltpu.make_async_copy(src, dst, lsem.at[k]))
        loads[-1].start()

    loads[0].wait()
    tw = tf[...].astype(F32)
    tu = tw / jnp.sqrt(jnp.sum(tw * tw, axis=1, keepdims=True) + EPS)
    teach[pi, 0:4, :] = tu[:, 0:128].astype(BF16).astype(F32)
    teach[pi, 4:8, :] = tu[:, 128:256].astype(BF16).astype(F32)
    loads[1].wait()
    sw = sf[...].astype(F32)
    sn = jnp.sqrt(jnp.sum(sw * sw, axis=1, keepdims=True) + EPS)
    sd = sw / sn
    snorm[...] = jnp.broadcast_to(sn, (OWN, 128))
    sdir[...] = sd
    pack[...] = jnp.zeros_like(pack)
    hsend[...] = jnp.zeros_like(hsend)
    pack[0:OWN, :] = sd[:, 0:128]
    pack[24 : 24 + OWN, :] = sd[:, 128:256]
    stud[py, pz] = pack[...].astype(BF16)

    loads[2].wait()

    @pl.loop(0, C // 256)
    def _(j):
        cols = pl.ds(pl.multiple_of(j * 256, 256), 256)
        v = tp[:, cols].astype(F32)
        inv = 1.0 / jnp.sqrt(jnp.sum(v * v, axis=0, keepdims=True) + EPS)
        tpb[:, cols] = (v * inv).astype(BF16)

    pl.semaphore_wait(barrier, NPR - 1 + NDP - 1)
    send(X_TEACH, "proto", teach)
    send(X_STUDZ, "z", stud.at[py])

    loads[3].wait()

    @pl.loop(0, C // 256)
    def _(j):
        cols = pl.ds(pl.multiple_of(j * 256, 256), 256)
        v = pr[:, cols].astype(F32)
        n = jnp.sqrt(jnp.sum(v * v, axis=0, keepdims=True) + EPS)
        pnorm[:, cols] = n
        wb[:, cols] = (v * (1.0 / n)).astype(BF16)

    loads[4].wait()
    loads[5].wait()
    lanes = lax.broadcasted_iota(jnp.int32, (128, 128), 1).astype(F32)
    base = (dp * IMG_DEV).astype(F32)
    for i in range(R // 128):
        image = row_to_columns(crop[i : i + 1, :].astype(F32)) - base
        w0 = row_to_columns(pair[0:1, 128 * i : 128 * i + 128].astype(F32))
        w1 = row_to_columns(pair[1:2, 128 * i : 128 * i + 128].astype(F32))
        sel = jnp.where(lanes == 2.0 * image, w0, 0.0) + jnp.where(lanes == 2.0 * image + 1.0, w1, 0.0)
        selb[128 * i : 128 * i + 128, :] = sel.astype(BF16)
        scalec[128 * i : 128 * i + 128, :] = w0 + w1
    own_rows = lax.broadcasted_iota(jnp.int32, (32, R), 0) + pi * OWN
    ownsel[...] = (lax.broadcasted_iota(jnp.int32, (32, R), 1) == own_rows).astype(F32)

    arrived(X_TEACH, "proto", teach)
    for p in range(NPR):
        v = teach[p]
        x32[4 * p : 4 * p + 4, 0:128] = v[0:4]
        x32[4 * p : 4 * p + 4, 128:256] = v[4:8]
    tgrp[dp] = x32[0:T, :].astype(BF16)

    def assign(g):
        rows = tgrp[g]
        for j in range(C // CH):
            e = jnp.exp(dot(rows, tpb[:, CH * j : CH * j + CH]) * TEACHER_SCALE)
            ass[group_rows(g), CH * j : CH * j + CH] = e

    assign(dp)

    def column_part(g, acc, arow, table=ass):
        if arow is not None:
            wide = row_to_columns(arow)
        for i in range(T // 8):
            e = table[pl.ds(pl.multiple_of(g * T + 8 * i, 8), 8), :]
            if arow is not None:
                e = e * jnp.concatenate([wide[8 * i : 8 * i + 8]] * (C // 128), axis=1)
            acc = acc + e
        return acc

    def row_part(g):
        cb = jnp.broadcast_to(cvec[...], (8, C))
        parts = []
        for i in range(T // 8):
            parts.append(lane_tiles(ass[pl.ds(pl.multiple_of(g * T + 8 * i, 8), 8), :] * cb))
        return columns_to_row(jnp.concatenate(parts, axis=0))

    col1[dp] = jnp.sum(column_part(dp, jnp.zeros((8, C), F32), None), axis=0, keepdims=True)
    send(X_COL1, "dp", col1)
    send(X_TGRP, "dp", tgrp)
    arrived(X_STUDZ, "z", stud.at[py])
    send(X_STUDY, "y", stud)

    arrived(X_COL1, "dp", col1)
    cvec[...] = 1.0 / jnp.sum(col1[...], axis=0)
    row1[pi] = row_part(dp)
    send(X_ROW1, "proto", row1)

    arrived(X_STUDY, "y", stud)
    for p in range(NPR):
        v = stud[p % 4, p // 4].astype(F32)
        x32[OWN * p : OWN * p + OWN, 0:128] = v[0:OWN]
        x32[OWN * p : OWN * p + OWN, 128:256] = v[24 : 24 + OWN]
    xb[...] = x32[...].astype(BF16)
    for i in range(R // 128):
        xt[:, 128 * i : 128 * i + 128] = jnp.transpose(x32[128 * i : 128 * i + 128, :]).astype(BF16)

    @pl.loop(0, R // 128)
    def _(i):
        rows = pl.ds(pl.multiple_of(i * 128, 128), 128)
        part = jnp.zeros((128, 128), F32)
        for j in range(C // CH):
            e = jnp.exp(dot(xb[rows, :], wb[:, CH * j : CH * j + CH]) * STUDENT_SCALE)
            expo[rows, CH * j : CH * j + CH] = e
            expb[rows, CH * j : CH * j + CH] = e.astype(BF16)
            part = part + lane_tiles(e)
        tot[pi, pl.ds(i, 1), :] = columns_to_row(part)

    tot[pi, 5:8, :] = jnp.ones((3, 128), F32)

    @pl.loop(0, R // 128)
    def _(i):
        rows = pl.ds(pl.multiple_of(i * 128, 128), 128)
        harr[rows, :] = dot_nt(expb[rows, :], wb[...])

    for p in range(NPR):
        for half in range(2):
            hsend[half, p % 4, p // 4, 0:OWN, :] = harr[OWN * p : OWN * p + OWN, 128 * half : 128 * half + 128]
    for half in range(2):
        hybuf[half, py] = hsend[half, py]

    arrived(X_ROW1, "proto", row1)
    avec[0:1, :] = 1.0 / jnp.sum(row1[...], axis=0)
    col2[dp] = jnp.sum(column_part(dp, jnp.zeros((8, C), F32), avec[0:1, :]), axis=0, keepdims=True)
    send(X_COL2, "dp", col2)
    send(X_HY0, "y", hybuf.at[0], hsend.at[0])
    send(X_TOT, "proto", tot)

    def half_sums(half, x, y):
        arrived(x, "y", hybuf.at[half])
        for z in range(8):
            hzsend[half, z] = jnp.sum(hybuf[half, :, z], axis=0)
        send(y, "z", hzbuf.at[half], hzsend.at[half])
        hzbuf[half, pz] = hzsend[half, pz]

    arrived(X_TGRP, "dp", tgrp)

    @pl.loop(1, NDP)
    def _(i):
        assign(lax.rem(dp + i, NDP))

    def columns():
        acc = jnp.zeros((8, C), F32)
        for g in range(NDP):
            acc = column_part(g, acc, avec[g : g + 1, :])
        cvec[...] = 1.0 / jnp.sum(acc, axis=0, keepdims=True)

    def rows_into(buf):
        buf[pi] = jnp.concatenate([row_part(g) for g in range(NDP)], axis=0)

    arrived(X_COL2, "dp", col2)
    cvec[...] = 1.0 / jnp.sum(col2[...], axis=0)
    rows_into(row2)
    send(X_ROW2, "proto", row2)
    send(X_HY1, "y", hybuf.at[1], hsend.at[1])

    half_sums(0, X_HY0, X_HZ0)

    ut = dot(xt[...], selb[...])
    for g in range(NDP):
        utsend[g] = ut[32 * g : 32 * g + 32, :]
    send(X_UT, "dp", utbuf, utsend)
    utbuf[dp] = utsend[dp]

    arrived(X_TOT, "proto", tot)
    inv_tot = 1.0 / jnp.sum(tot[...], axis=0)
    for i in range(R // 128):
        rows = slice(128 * i, 128 * i + 128)
        scalec[rows, :] = scalec[rows, :] * row_to_columns(inv_tot[i : i + 1, :])

    @pl.loop(0, R // 16)
    def _(i):
        rows = pl.ds(pl.multiple_of(i * 16, 16), 16)
        s = scalec[rows, :]
        probb[rows, :] = (expo[rows, :] * jnp.concatenate([s] * (C // 128), axis=1)).astype(BF16)

    for j in range(C // CH):
        cols = slice(CH * j, CH * j + CH)
        pg = dot(xt[...], probb[:, cols])
        direction = pr[:, cols].astype(F32) / pnorm[:, cols]
        pg = (pg - direction * jnp.sum(direction * pg, axis=0, keepdims=True)).astype(BF16)
        for g in range(NDP):
            pgsend[g, :, cols] = pg[32 * g : 32 * g + 32, :]
    send(X_PG, "dp", pgbuf, pgsend)
    pgbuf[dp] = pgsend[dp]

    ur = jnp.transpose(ut)
    utb = ur.astype(BF16)
    utb = jnp.concatenate([utb, (ur - utb.astype(F32)).astype(BF16)], axis=0)
    for j in range(C // CH):
        cols = slice(CH * j, CH * j + CH)
        along = dot(utb, wb[:, cols])
        along = along[0:T] + along[T : 2 * T]
        mown[:, cols] = along * ass[group_rows(dp), cols].astype(BF16).astype(F32)

    arrived(X_ROW2, "proto", row2)
    avec[...] = 1.0 / jnp.sum(row2[...], axis=0)
    columns()

    cb = jnp.broadcast_to(cvec[...], (16, C))
    for i in range(T // 16):
        rows = pl.ds(pl.multiple_of(dp * T + 16 * i, 16), 16)
        probb[16 * i : 16 * i + 16, :] = (ass[rows, :] * cb).astype(BF16)
    garr[...] = dot_nt(probb[0:T, :], wb[...])
    for p in range(16):
        gsend[p] = garr[8 * p : 8 * p + 8, 0:128]
        gsend[p + 16] = garr[8 * p : 8 * p + 8, 128:256]
    send(X_G, "proto", gbuf, gsend)
    half_sums(1, X_HY1, X_HZ1)
    gbuf[pi] = gsend[pi]
    rows_into(row3)
    send(X_ROW3, "proto", row3)


    arrived(X_HZ0, "z", hzbuf.at[0])
    arrived(X_HZ1, "z", hzbuf.at[1])
    hsum = jnp.sum(hzbuf[...], axis=1)
    own_scale = jnp.dot(ownsel[...], scalec[...], precision=lax.Precision.HIGHEST, preferred_element_type=F32)[0:OWN, 0:1]
    own_pick = dot(ownsel[...].astype(BF16), selb[...])[0:OWN, :]

    @pl.loop(0, NDP * T // 32)
    def _(i):
        rows = pl.ds(pl.multiple_of(i * 32, 32), 32)
        assb[rows, :] = ass[rows, :].astype(BF16)

    arrived(X_G, "proto", gbuf)
    gall[pi] = jnp.sum(gbuf[...], axis=0)
    send(X_GALL, "proto", gall)

    arrived(X_ROW3, "proto", row3)
    avec[...] = 1.0 / jnp.sum(row3[...], axis=0)
    along = jnp.sum(column_part(0, jnp.zeros((8, C), F32), avec[pl.ds(dp, 1), :], mown), axis=0, keepdims=True)
    dotbuf[dp] = along * cvec[...]
    send(X_DOT, "dp", dotbuf)
    arrived(X_UT, "dp", utbuf)
    lhs = jnp.concatenate([utbuf[g] * avec[g : g + 1, :] for g in range(NDP)], axis=1)
    high = lhs.astype(BF16)
    lhs = jnp.concatenate([high, (lhs - high.astype(F32)).astype(BF16)], axis=0)
    arrived(X_PG, "dp", pgbuf)
    own32 = pl.ds(pl.multiple_of(dp * 32, 32), 32)
    for j in range(C // CH):
        cols = slice(CH * j, CH * j + CH)
        both = dot(lhs, assb[:, cols])
        target = (both[0:32] + both[32:64]) * cvec[:, cols]
        own = GRAD_SCALE * (jnp.sum(pgbuf[:, :, cols].astype(F32), axis=0) - target)
        pown[:, cols] = own

    arrived(X_DOT, "dp", dotbuf)
    for j in range(C // CH):
        cols = slice(CH * j, CH * j + CH)
        column_dot = -GRAD_SCALE * jnp.sum(dotbuf[:, :, cols], axis=0)
        inv = 1.0 / pnorm[:, cols]
        pown[:, cols] = (pown[:, cols] - pr[own32, cols].astype(F32) * (inv * column_dot)) * inv
    store = pltpu.make_async_copy(pown, pgrad, lsem.at[6])
    store.start()

    arrived(X_GALL, "proto", gall)
    gfull = jnp.concatenate([gall[0:16].reshape(T, 128), gall[16:32].reshape(T, 128)], axis=1)
    picked = jnp.dot(
        own_pick * avec[pl.ds(dp, 1), :], gfull, precision=lax.Precision.HIGHEST, preferred_element_type=F32
    )
    h = jnp.concatenate([hsum[0, 0:OWN], hsum[1, 0:OWN]], axis=1)
    unit_grad = GRAD_SCALE * (own_scale * h - picked)
    sd = sdir[...]
    sgrad[...] = (unit_grad - sd * jnp.sum(sd * unit_grad, axis=1, keepdims=True)) / snorm[:, 0:1]

    store.wait()
    for x, axis, buf in (
        (X_TEACH, "proto", teach), (X_STUDZ, "z", stud.at[py]), (X_STUDY, "y", stud), (X_COL1, "dp", col1),
        (X_TGRP, "dp", tgrp), (X_ROW1, "proto", row1), (X_COL2, "dp", col2), (X_TOT, "proto", tot),
        (X_ROW2, "proto", row2), (X_HY0, "y", hybuf.at[0]), (X_HY1, "y", hybuf.at[1]),
        (X_HZ0, "z", hzbuf.at[0]), (X_HZ1, "z", hzbuf.at[1]), (X_UT, "dp", utbuf), (X_ROW3, "proto", row3),
        (X_G, "proto", gbuf), (X_PG, "dp", pgbuf), (X_GALL, "proto", gall), (X_DOT, "dp", dotbuf),
    ):
        sent(x, axis, buf)


def last_step(student, proto, sgrad, pgrad):
    sgrad[...] = student[...]
    pgrad[...] = proto[...]


def per_device(student_feats, teacher_feats, prototypes, teacher_prototypes, crop_image, pairing):
    vmem = pl.BlockSpec(memory_space=pltpu.VMEM)
    anywhere = pl.BlockSpec(memory_space=pl.ANY)
    outs = (jax.ShapeDtypeStruct((OWN, K), F32), jax.ShapeDtypeStruct((K // NDP, C), F32))
    student, proto = pl.pallas_call(
        kernel,
        out_shape=outs,
        in_specs=[anywhere] * 6,
        out_specs=(vmem, anywhere),
        scratch_shapes=[
            pltpu.VMEM((NPR, 8, 128), F32),
            pltpu.VMEM((4, 8, PAD, 128), BF16),
            pltpu.VMEM((NDP, 1, C), F32),
            pltpu.VMEM((NDP, T, K), BF16),
            pltpu.VMEM((NPR, 1, 128), F32),
            pltpu.VMEM((NDP, 1, C), F32),
            pltpu.VMEM((NPR, 8, 128), F32),
            pltpu.VMEM((NPR, 8, 128), F32),
            pltpu.VMEM((2, 4, 8, HPAD, 128), F32),
            pltpu.VMEM((2, 8, HPAD, 128), F32),
            pltpu.VMEM((NDP, 32, 128), F32),
            pltpu.VMEM((NPR, 8, 128), F32),
            pltpu.VMEM((NPR, 8, 128), F32),
            pltpu.VMEM((NDP, 32, C), BF16),
            pltpu.VMEM((NPR, 8, 128), F32),
            pltpu.VMEM((NDP, 1, C), F32),
            pltpu.VMEM((2, 4, 8, HPAD, 128), F32),
            pltpu.VMEM((2, 8, HPAD, 128), F32),
            pltpu.VMEM((NDP, 32, 128), F32),
            pltpu.VMEM((NPR, 8, 128), F32),
            pltpu.VMEM((NDP, 32, C), BF16),
            pltpu.VMEM((PAD, 128), F32),
            pltpu.VMEM((R, K), F32),
            pltpu.VMEM((R, K), BF16),
            pltpu.VMEM((K, R), BF16),
            pltpu.VMEM((K, C), BF16),
            pltpu.VMEM((K, C), BF16),
            pltpu.VMEM((1, C), F32),
            pltpu.VMEM((K // NDP, C), F32),
            pltpu.VMEM((R, C), F32),
            pltpu.VMEM((R, C), BF16),
            pltpu.VMEM((R, C), BF16),
            pltpu.VMEM((R, 128), BF16),
            pltpu.VMEM((R, 128), F32),
            pltpu.VMEM((R, K), F32),
            pltpu.VMEM((T, K), F32),
            pltpu.VMEM((NDP * T, C), F32),
            pltpu.VMEM((NDP * T, C), BF16),
            pltpu.VMEM((T, C), F32),
            pltpu.VMEM((1, C), F32),
            pltpu.VMEM((8, 128), F32),
            pltpu.VMEM((OWN, K), F32),
            pltpu.VMEM((OWN, 128), F32),
            pltpu.VMEM((32, R), F32),
            pltpu.VMEM((OWN, K), BF16),
            pltpu.VMEM((4, K), BF16),
            pltpu.VMEM((K, C), BF16),
            pltpu.VMEM((K, C), BF16),
            pltpu.VMEM((R // 128, 128), jnp.int32),
            pltpu.VMEM((2, R), jnp.int32),
            pltpu.SemaphoreType.DMA((N_X,)),
            pltpu.SemaphoreType.DMA((N_X,)),
            pltpu.SemaphoreType.DMA((7,)),
        ],
        compiler_params=pltpu.CompilerParams(
            collective_id=0, has_side_effects=True, vmem_limit_bytes=56 * 2**20
        ),
    )(student_feats, teacher_feats, prototypes, teacher_prototypes, crop_image.reshape(R // 128, 128), pairing.T)
    return pl.pallas_call(
        last_step,
        out_shape=outs,
        in_specs=[vmem] * 2,
        out_specs=(vmem, vmem),
        compiler_params=pltpu.CompilerParams(vmem_limit_bytes=56 * 2**20),
    )(student, proto)


def solution(mesh):
    in_specs = (
        P(("dp", "proto"), None),
        P(("dp", "proto"), None),
        P(None, "proto"),
        P(None, "proto"),
        P("dp"),
        P("dp", None),
    )
    out_specs = (P(("dp", "proto"), None), P("dp", "proto"))
    return jax.shard_map(
        per_device, mesh=mesh, in_specs=in_specs, out_specs=out_specs, check_vma=False
    )
```

```python
import jax
import jax.numpy as jnp
from jax import lax
from jax.experimental import pallas as pl
from jax.experimental.pallas import tpu as pltpu
from jax.sharding import PartitionSpec as P

MESH = pl.DeviceIdType.MESH
F32 = jnp.float32
BF16 = jnp.bfloat16

IMG_DEV = 64
EPS = 1e-06
TEACHER_SCALE = 1.0 / 0.07
STUDENT_SCALE = 1.0 / 0.1
GRAD_SCALE = 4096.0 / 0.1

NDP = 8
NPR = 32
K = 256
C = 2048
R = 640
T = 128
OWN = 20
PAD = 48
HPAD = 24
CH = 512

(
    X_TEACH, X_STUDZ, X_STUDY, X_COL1, X_TGRP, X_ROW1, X_COL2, X_TOT, X_ROW2, X_HY0, X_HY1, X_HZ0, X_HZ1, X_UT, X_ROW3, X_G, X_PG, X_GALL, X_DOT
) = range(19)
N_X = 19
SIZES = {"dp": 8, "proto": 32, "z": 8, "y": 4}


def row_to_columns(row):
    return jnp.transpose(jnp.broadcast_to(row, (128, 128)))


def columns_to_row(part):
    return jnp.sum(jnp.transpose(part), axis=0, keepdims=True)


def lane_tiles(value):
    total = value[:, 0:128]
    for j in range(1, value.shape[1] // 128):
        total = total + value[:, 128 * j : 128 * j + 128]
    return total


def dot(a, b):
    return jnp.dot(a, b, preferred_element_type=F32)


def dot_nt(a, b):
    return lax.dot_general(a, b, (((1,), (1,)), ((), ())), preferred_element_type=F32)


def kernel(
    sfh, tfh, prh, tph, croph, pairh,
    sgrad, pgrad,
    teach, stud, col1, tgrp, row1, col2, tot, row2, hybuf, hzbuf, utbuf, row3, gbuf, pgbuf, gall, dotbuf,
    hsend, hzsend, utsend, gsend, pgsend,
    pack, x32, xb, xt, wb, tpb, pnorm, pown, expo, expb, probb, selb, scalec, harr, garr, ass, assb, mown, cvec, avec,
    sdir, snorm, ownsel, sf, tf, pr, tp, crop, pair,
    ssem, rsem, lsem,
):
    dp = lax.axis_index("dp")
    pi = lax.axis_index("proto")

    pz, py = pi // 4, lax.rem(pi, 4)

    def far_first(i, half):
        return half + ((i + 1) // 2) * (1 - 2 * lax.rem(i, 2))

    def peer(axis, i):
        if axis == "dp":
            return lax.rem(dp + i + 1, NDP)
        if axis == "z":
            return lax.rem(pz + far_first(i, 4), 8)
        if axis == "y":
            return lax.rem(py + far_first(i, 2), 4)
        return lax.rem(pz + far_first(i // 4, 4), 8) * 4 + lax.rem(py + far_first(lax.rem(i, 4), 2), 4)

    def address(axis, p):
        if axis == "dp":
            return (p, pi)
        if axis == "z":
            return (dp, p * 4 + py)
        if axis == "y":
            return (dp, pz * 4 + p)
        return (dp, p)

    def mine(axis):
        return {"dp": dp, "proto": pi, "z": pz, "y": py}[axis]

    def count(axis):
        return SIZES[axis]

    def send(x, axis, dst, src=None):
        me = mine(axis)

        @pl.loop(0, count(axis) - 1)
        def _(i):
            p = peer(axis, i)
            pltpu.make_async_remote_copy(
                src_ref=dst.at[me] if src is None else src.at[p],
                dst_ref=dst.at[me],
                send_sem=ssem.at[x],
                recv_sem=rsem.at[x],
                device_id=address(axis, p),
                device_id_type=MESH,
            ).start()

    def arrived(x, axis, dst):
        blocks = dst.at[pl.ds(0, count(axis) - 1)]
        pltpu.make_async_copy(blocks, blocks, rsem.at[x]).wait()

    def sent(x, axis, dst):
        blocks = dst.at[pl.ds(0, count(axis) - 1)]
        pltpu.make_async_copy(blocks, blocks, ssem.at[x]).wait()

    def group_rows(g):
        return pl.ds(pl.multiple_of(g * T, T), T)

    barrier = pltpu.get_barrier_semaphore()
    for axis in ("proto", "dp"):
        @pl.loop(0, count(axis) - 1)
        def _(i, axis=axis):
            p = peer(axis, i)
            pl.semaphore_signal(barrier, inc=1, device_id=address(axis, p), device_id_type=MESH)

    loads = []
    for k, (src, dst) in enumerate(
        ((tfh, tf), (sfh, sf), (tph, tp), (prh, pr), (croph, crop), (pairh, pair))
    ):
        loads.append(pltpu.make_async_copy(src, dst, lsem.at[k]))
        loads[-1].start()

    loads[0].wait()
    tw = tf[...].astype(F32)
    tu = tw / jnp.sqrt(jnp.sum(tw * tw, axis=1, keepdims=True) + EPS)
    teach[pi, 0:4, :] = tu[:, 0:128].astype(BF16).astype(F32)
    teach[pi, 4:8, :] = tu[:, 128:256].astype(BF16).astype(F32)
    loads[1].wait()
    sw = sf[...].astype(F32)
    sn = jnp.sqrt(jnp.sum(sw * sw, axis=1, keepdims=True) + EPS)
    sd = sw / sn
    snorm[...] = jnp.broadcast_to(sn, (OWN, 128))
    sdir[...] = sd
    pack[...] = jnp.zeros_like(pack)
    hsend[...] = jnp.zeros_like(hsend)
    pack[0:OWN, :] = sd[:, 0:128]
    pack[24 : 24 + OWN, :] = sd[:, 128:256]
    stud[py, pz] = pack[...].astype(BF16)

    loads[2].wait()

    @pl.loop(0, C // 256)
    def _(j):
        cols = pl.ds(pl.multiple_of(j * 256, 256), 256)
        v = tp[:, cols].astype(F32)
        inv = 1.0 / jnp.sqrt(jnp.sum(v * v, axis=0, keepdims=True) + EPS)
        tpb[:, cols] = (v * inv).astype(BF16)

    pl.semaphore_wait(barrier, NPR - 1 + NDP - 1)
    send(X_TEACH, "proto", teach)
    send(X_STUDZ, "z", stud.at[py])

    loads[3].wait()

    @pl.loop(0, C // 256)
    def _(j):
        cols = pl.ds(pl.multiple_of(j * 256, 256), 256)
        v = pr[:, cols].astype(F32)
        n = jnp.sqrt(jnp.sum(v * v, axis=0, keepdims=True) + EPS)
        pnorm[:, cols] = n
        wb[:, cols] = (v * (1.0 / n)).astype(BF16)

    arrived(X_TEACH, "proto", teach)
    for p in range(NPR):
        v = teach[p]
        x32[4 * p : 4 * p + 4, 0:128] = v[0:4]
        x32[4 * p : 4 * p + 4, 128:256] = v[4:8]
    tgrp[dp] = x32[0:T, :].astype(BF16)

    def assign(g):
        rows = tgrp[g]
        for j in range(C // CH):
            e = jnp.exp(dot(rows, tpb[:, CH * j : CH * j + CH]) * TEACHER_SCALE)
            ass[group_rows(g), CH * j : CH * j + CH] = e

    assign(dp)

    def column_part(g, acc, arow, table=ass):
        if arow is not None:
            wide = row_to_columns(arow)
        for i in range(T // 8):
            e = table[pl.ds(pl.multiple_of(g * T + 8 * i, 8), 8), :]
            if arow is not None:
                e = e * jnp.concatenate([wide[8 * i : 8 * i + 8]] * (C // 128), axis=1)
            acc = acc + e
        return acc

    def row_part(g):
        cb = jnp.broadcast_to(cvec[...], (8, C))
        parts = []
        for i in range(T // 8):
            parts.append(lane_tiles(ass[pl.ds(pl.multiple_of(g * T + 8 * i, 8), 8), :] * cb))
        return columns_to_row(jnp.concatenate(parts, axis=0))

    col1[dp] = jnp.sum(column_part(dp, jnp.zeros((8, C), F32), None), axis=0, keepdims=True)
    send(X_COL1, "dp", col1)
    send(X_TGRP, "dp", tgrp)
    arrived(X_STUDZ, "z", stud.at[py])
    send(X_STUDY, "y", stud)

    loads[4].wait()
    loads[5].wait()
    lanes = lax.broadcasted_iota(jnp.int32, (128, 128), 1).astype(F32)
    base = (dp * IMG_DEV).astype(F32)
    for i in range(R // 128):
        image = row_to_columns(crop[i : i + 1, :].astype(F32)) - base
        w0 = row_to_columns(pair[0:1, 128 * i : 128 * i + 128].astype(F32))
        w1 = row_to_columns(pair[1:2, 128 * i : 128 * i + 128].astype(F32))
        sel = jnp.where(lanes == 2.0 * image, w0, 0.0) + jnp.where(lanes == 2.0 * image + 1.0, w1, 0.0)
        selb[128 * i : 128 * i + 128, :] = sel.astype(BF16)
        scalec[128 * i : 128 * i + 128, :] = w0 + w1
    own_rows = lax.broadcasted_iota(jnp.int32, (32, R), 0) + pi * OWN
    ownsel[...] = (lax.broadcasted_iota(jnp.int32, (32, R), 1) == own_rows).astype(F32)

    arrived(X_COL1, "dp", col1)
    cvec[...] = 1.0 / jnp.sum(col1[...], axis=0)
    row1[pi] = row_part(dp)
    send(X_ROW1, "proto", row1)

    arrived(X_STUDY, "y", stud)
    for p in range(NPR):
        v = stud[p % 4, p // 4].astype(F32)
        x32[OWN * p : OWN * p + OWN, 0:128] = v[0:OWN]
        x32[OWN * p : OWN * p + OWN, 128:256] = v[24 : 24 + OWN]
    xb[...] = x32[...].astype(BF16)
    for i in range(R // 128):
        xt[:, 128 * i : 128 * i + 128] = jnp.transpose(x32[128 * i : 128 * i + 128, :]).astype(BF16)

    @pl.loop(0, R // 128)
    def _(i):
        rows = pl.ds(pl.multiple_of(i * 128, 128), 128)
        part = jnp.zeros((128, 128), F32)
        for j in range(C // CH):
            e = jnp.exp(dot(xb[rows, :], wb[:, CH * j : CH * j + CH]) * STUDENT_SCALE)
            expo[rows, CH * j : CH * j + CH] = e
            expb[rows, CH * j : CH * j + CH] = e.astype(BF16)
            part = part + lane_tiles(e)
        tot[pi, pl.ds(i, 1), :] = columns_to_row(part)

    tot[pi, 5:8, :] = jnp.ones((3, 128), F32)

    @pl.loop(0, R // 128)
    def _(i):
        rows = pl.ds(pl.multiple_of(i * 128, 128), 128)
        harr[rows, :] = dot_nt(expb[rows, :], wb[...])

    for p in range(NPR):
        for half in range(2):
            hsend[half, p % 4, p // 4, 0:OWN, :] = harr[OWN * p : OWN * p + OWN, 128 * half : 128 * half + 128]
    for half in range(2):
        hybuf[half, py] = hsend[half, py]

    arrived(X_ROW1, "proto", row1)
    avec[0:1, :] = 1.0 / jnp.sum(row1[...], axis=0)
    col2[dp] = jnp.sum(column_part(dp, jnp.zeros((8, C), F32), avec[0:1, :]), axis=0, keepdims=True)
    send(X_COL2, "dp", col2)
    send(X_HY0, "y", hybuf.at[0], hsend.at[0])
    send(X_TOT, "proto", tot)

    def half_sums(half, x, y):
        arrived(x, "y", hybuf.at[half])
        for z in range(8):
            hzsend[half, z] = jnp.sum(hybuf[half, :, z], axis=0)
        send(y, "z", hzbuf.at[half], hzsend.at[half])
        hzbuf[half, pz] = hzsend[half, pz]

    arrived(X_TGRP, "dp", tgrp)

    @pl.loop(1, NDP)
    def _(i):
        assign(lax.rem(dp + i, NDP))

    def columns():
        acc = jnp.zeros((8, C), F32)
        for g in range(NDP):
            acc = column_part(g, acc, avec[g : g + 1, :])
        cvec[...] = 1.0 / jnp.sum(acc, axis=0, keepdims=True)

    def rows_into(buf):
        buf[pi] = jnp.concatenate([row_part(g) for g in range(NDP)], axis=0)

    arrived(X_COL2, "dp", col2)
    cvec[...] = 1.0 / jnp.sum(col2[...], axis=0)
    rows_into(row2)
    send(X_ROW2, "proto", row2)
    send(X_HY1, "y", hybuf.at[1], hsend.at[1])

    half_sums(0, X_HY0, X_HZ0)

    ut = dot(xt[...], selb[...])
    for g in range(NDP):
        utsend[g] = ut[32 * g : 32 * g + 32, :]
    send(X_UT, "dp", utbuf, utsend)
    utbuf[dp] = utsend[dp]

    arrived(X_TOT, "proto", tot)
    inv_tot = 1.0 / jnp.sum(tot[...], axis=0)
    for i in range(R // 128):
        rows = slice(128 * i, 128 * i + 128)
        scalec[rows, :] = scalec[rows, :] * row_to_columns(inv_tot[i : i + 1, :])

    @pl.loop(0, R // 16)
    def _(i):
        rows = pl.ds(pl.multiple_of(i * 16, 16), 16)
        s = scalec[rows, :]
        probb[rows, :] = (expo[rows, :] * jnp.concatenate([s] * (C // 128), axis=1)).astype(BF16)

    for j in range(C // CH):
        cols = slice(CH * j, CH * j + CH)
        pg = dot(xt[...], probb[:, cols])
        direction = pr[:, cols].astype(F32) / pnorm[:, cols]
        pg = (pg - direction * jnp.sum(direction * pg, axis=0, keepdims=True)).astype(BF16)
        for g in range(NDP):
            pgsend[g, :, cols] = pg[32 * g : 32 * g + 32, :]
    send(X_PG, "dp", pgbuf, pgsend)
    pgbuf[dp] = pgsend[dp]

    ur = jnp.transpose(ut)
    utb = ur.astype(BF16)
    utb = jnp.concatenate([utb, (ur - utb.astype(F32)).astype(BF16)], axis=0)
    for j in range(C // CH):
        cols = slice(CH * j, CH * j + CH)
        along = dot(utb, wb[:, cols])
        along = along[0:T] + along[T : 2 * T]
        mown[:, cols] = along * ass[group_rows(dp), cols].astype(BF16).astype(F32)

    arrived(X_ROW2, "proto", row2)
    avec[...] = 1.0 / jnp.sum(row2[...], axis=0)
    columns()

    cb = jnp.broadcast_to(cvec[...], (16, C))
    for i in range(T // 16):
        rows = pl.ds(pl.multiple_of(dp * T + 16 * i, 16), 16)
        probb[16 * i : 16 * i + 16, :] = (ass[rows, :] * cb).astype(BF16)
    garr[...] = dot_nt(probb[0:T, :], wb[...])
    for p in range(16):
        gsend[p] = garr[8 * p : 8 * p + 8, 0:128]
        gsend[p + 16] = garr[8 * p : 8 * p + 8, 128:256]
    send(X_G, "proto", gbuf, gsend)
    half_sums(1, X_HY1, X_HZ1)
    gbuf[pi] = gsend[pi]
    rows_into(row3)
    send(X_ROW3, "proto", row3)


    arrived(X_HZ0, "z", hzbuf.at[0])
    arrived(X_HZ1, "z", hzbuf.at[1])
    hsum = jnp.sum(hzbuf[...], axis=1)
    own_scale = jnp.dot(ownsel[...], scalec[...], precision=lax.Precision.HIGHEST, preferred_element_type=F32)[0:OWN, 0:1]
    own_pick = dot(ownsel[...].astype(BF16), selb[...])[0:OWN, :]

    @pl.loop(0, NDP * T // 32)
    def _(i):
        rows = pl.ds(pl.multiple_of(i * 32, 32), 32)
        assb[rows, :] = ass[rows, :].astype(BF16)

    arrived(X_G, "proto", gbuf)
    gall[pi] = jnp.sum(gbuf[...], axis=0)
    send(X_GALL, "proto", gall)

    arrived(X_ROW3, "proto", row3)
    avec[...] = 1.0 / jnp.sum(row3[...], axis=0)
    along = jnp.sum(column_part(0, jnp.zeros((8, C), F32), avec[pl.ds(dp, 1), :], mown), axis=0, keepdims=True)
    dotbuf[dp] = along * cvec[...]
    send(X_DOT, "dp", dotbuf)
    arrived(X_UT, "dp", utbuf)
    lhs = jnp.concatenate([utbuf[g] * avec[g : g + 1, :] for g in range(NDP)], axis=1)
    high = lhs.astype(BF16)
    lhs = jnp.concatenate([high, (lhs - high.astype(F32)).astype(BF16)], axis=0)
    arrived(X_PG, "dp", pgbuf)
    own32 = pl.ds(pl.multiple_of(dp * 32, 32), 32)
    for j in range(C // CH):
        cols = slice(CH * j, CH * j + CH)
        both = dot(lhs, assb[:, cols])
        target = (both[0:32] + both[32:64]) * cvec[:, cols]
        own = GRAD_SCALE * (jnp.sum(pgbuf[:, :, cols].astype(F32), axis=0) - target)
        pown[:, cols] = own

    arrived(X_DOT, "dp", dotbuf)
    for j in range(C // CH):
        cols = slice(CH * j, CH * j + CH)
        column_dot = -GRAD_SCALE * jnp.sum(dotbuf[:, :, cols], axis=0)
        inv = 1.0 / pnorm[:, cols]
        pown[:, cols] = (pown[:, cols] - pr[own32, cols].astype(F32) * (inv * column_dot)) * inv
    store = pltpu.make_async_copy(pown, pgrad, lsem.at[6])
    store.start()

    arrived(X_GALL, "proto", gall)
    gfull = jnp.concatenate([gall[0:16].reshape(T, 128), gall[16:32].reshape(T, 128)], axis=1)
    picked = jnp.dot(
        own_pick * avec[pl.ds(dp, 1), :], gfull, precision=lax.Precision.HIGHEST, preferred_element_type=F32
    )
    h = jnp.concatenate([hsum[0, 0:OWN], hsum[1, 0:OWN]], axis=1)
    unit_grad = GRAD_SCALE * (own_scale * h - picked)
    sd = sdir[...]
    sgrad[...] = (unit_grad - sd * jnp.sum(sd * unit_grad, axis=1, keepdims=True)) / snorm[:, 0:1]

    store.wait()
    for x, axis, buf in (
        (X_TEACH, "proto", teach), (X_STUDZ, "z", stud.at[py]), (X_STUDY, "y", stud), (X_COL1, "dp", col1),
        (X_TGRP, "dp", tgrp), (X_ROW1, "proto", row1), (X_COL2, "dp", col2), (X_TOT, "proto", tot),
        (X_ROW2, "proto", row2), (X_HY0, "y", hybuf.at[0]), (X_HY1, "y", hybuf.at[1]),
        (X_HZ0, "z", hzbuf.at[0]), (X_HZ1, "z", hzbuf.at[1]), (X_UT, "dp", utbuf), (X_ROW3, "proto", row3),
        (X_G, "proto", gbuf), (X_PG, "dp", pgbuf), (X_GALL, "proto", gall), (X_DOT, "dp", dotbuf),
    ):
        sent(x, axis, buf)


def last_step(student, proto, sgrad, pgrad):
    sgrad[...] = student[...]
    pgrad[...] = proto[...]


def per_device(student_feats, teacher_feats, prototypes, teacher_prototypes, crop_image, pairing):
    vmem = pl.BlockSpec(memory_space=pltpu.VMEM)
    anywhere = pl.BlockSpec(memory_space=pl.ANY)
    outs = (jax.ShapeDtypeStruct((OWN, K), F32), jax.ShapeDtypeStruct((K // NDP, C), F32))
    student, proto = pl.pallas_call(
        kernel,
        out_shape=outs,
        in_specs=[anywhere] * 6,
        out_specs=(vmem, anywhere),
        scratch_shapes=[
            pltpu.VMEM((NPR, 8, 128), F32),
            pltpu.VMEM((4, 8, PAD, 128), BF16),
            pltpu.VMEM((NDP, 1, C), F32),
            pltpu.VMEM((NDP, T, K), BF16),
            pltpu.VMEM((NPR, 1, 128), F32),
            pltpu.VMEM((NDP, 1, C), F32),
            pltpu.VMEM((NPR, 8, 128), F32),
            pltpu.VMEM((NPR, 8, 128), F32),
            pltpu.VMEM((2, 4, 8, HPAD, 128), F32),
            pltpu.VMEM((2, 8, HPAD, 128), F32),
            pltpu.VMEM((NDP, 32, 128), F32),
            pltpu.VMEM((NPR, 8, 128), F32),
            pltpu.VMEM((NPR, 8, 128), F32),
            pltpu.VMEM((NDP, 32, C), BF16),
            pltpu.VMEM((NPR, 8, 128), F32),
            pltpu.VMEM((NDP, 1, C), F32),
            pltpu.VMEM((2, 4, 8, HPAD, 128), F32),
            pltpu.VMEM((2, 8, HPAD, 128), F32),
            pltpu.VMEM((NDP, 32, 128), F32),
            pltpu.VMEM((NPR, 8, 128), F32),
            pltpu.VMEM((NDP, 32, C), BF16),
            pltpu.VMEM((PAD, 128), F32),
            pltpu.VMEM((R, K), F32),
            pltpu.VMEM((R, K), BF16),
            pltpu.VMEM((K, R), BF16),
            pltpu.VMEM((K, C), BF16),
            pltpu.VMEM((K, C), BF16),
            pltpu.VMEM((1, C), F32),
            pltpu.VMEM((K // NDP, C), F32),
            pltpu.VMEM((R, C), F32),
            pltpu.VMEM((R, C), BF16),
            pltpu.VMEM((R, C), BF16),
            pltpu.VMEM((R, 128), BF16),
            pltpu.VMEM((R, 128), F32),
            pltpu.VMEM((R, K), F32),
            pltpu.VMEM((T, K), F32),
            pltpu.VMEM((NDP * T, C), F32),
            pltpu.VMEM((NDP * T, C), BF16),
            pltpu.VMEM((T, C), F32),
            pltpu.VMEM((1, C), F32),
            pltpu.VMEM((8, 128), F32),
            pltpu.VMEM((OWN, K), F32),
            pltpu.VMEM((OWN, 128), F32),
            pltpu.VMEM((32, R), F32),
            pltpu.VMEM((OWN, K), BF16),
            pltpu.VMEM((4, K), BF16),
            pltpu.VMEM((K, C), BF16),
            pltpu.VMEM((K, C), BF16),
            pltpu.VMEM((R // 128, 128), jnp.int32),
            pltpu.VMEM((2, R), jnp.int32),
            pltpu.SemaphoreType.DMA((N_X,)),
            pltpu.SemaphoreType.DMA((N_X,)),
            pltpu.SemaphoreType.DMA((7,)),
        ],
        compiler_params=pltpu.CompilerParams(
            collective_id=0, has_side_effects=True, vmem_limit_bytes=56 * 2**20
        ),
    )(student_feats, teacher_feats, prototypes, teacher_prototypes, crop_image.reshape(R // 128, 128), pairing.T)
    return pl.pallas_call(
        last_step,
        out_shape=outs,
        in_specs=[vmem] * 2,
        out_specs=(vmem, vmem),
        compiler_params=pltpu.CompilerParams(vmem_limit_bytes=56 * 2**20),
    )(student, proto)


def solution(mesh):
    in_specs = (
        P(("dp", "proto"), None),
        P(("dp", "proto"), None),
        P(None, "proto"),
        P(None, "proto"),
        P("dp"),
        P("dp", None),
    )
    out_specs = (P(("dp", "proto"), None), P("dp", "proto"))
    return jax.shard_map(
        per_device, mesh=mesh, in_specs=in_specs, out_specs=out_specs, check_vma=False
    )
```
